32 devices in a mesh: head: 4 (over y, x), blk: 8 (over z, core).
Axes of the slice: x: 2, y: 2, z: 4, core: 2. Of those that a mesh axis runs over, the one named last changes fastest.
Arguments:
- doc_x: bfloat16 [8192, 1024], P('blk'), may hold values from -6 to 6
- doc_seg: int32 [8192], P('blk'), may hold values from 0 to 127, as said below
- doc_query: int32 [128], replicated, may hold values from 0 to 7
- doc_var: int32 [8192], P('blk'), may hold values from 0 to 7
- query_len: int32 [8], replicated, may hold values from 256 to 512, as said below
- block_perm: int32 [8], replicated, may hold values from 0 to 7, each once
- cache_k: bfloat16 [4096, 1024], P('blk', 'head'), may hold values from -164 to 164
- cache_v: bfloat16 [4096, 1024], P('blk', 'head'), may hold values from -6 to 6
- cache_var: int32 [4096], P('blk'), may hold values from 0 to 7
- w_query: bfloat16 [1024, 1024], P(None, 'head'), may hold values from -0.1875 to 0.1875
- w_key: bfloat16 [1024, 1024], P(None, 'head'), may hold values from -0.5 to 0.5
- w_value: bfloat16 [1024, 1024], P(None, 'head'), may hold values from -0.1875 to 0.1875
- w_out: bfloat16 [1024, 1024], P('head'), may hold values from -0.1875 to 0.1875
- var_bias: float32 [2, 16], P(None, 'head'), may hold values from -1 to 1
- norm_gain: float32 [1024], replicated, may hold values from 0.1 to 1.9
- readout: float32 [1024], replicated, may hold values from -1.5 to 1.5
Outputs:
- update: float32 [8192, 1024], P('blk', 'head')
- pooled: float32 [128], P('blk')
The draws below stay inside these ranges and needn't reach their ends.
Inputs may be any that keep to these rules, and one draw needn't show every extreme that they name: `doc_seg`: index i of blk holds documents i * 16 to (i + 1) * 16 - 1 whole; its 1024 tokens form 8 runs of 128 tokens, run j holding its documents 2j and 2j + 1, both of one query, and the 8 runs of one index belong to 8 different queries. query_len[0] = 512.
All inputs are finite; a program needn't handle non-finite values.
Results may differ from the reference program's by a relative error of at most 0.012.
The reference program's roundings to bfloat16 on the way (of `query_rot`, `key_rot`, `value_proj` and `attended`) count: a program that leaves them out, or rounds other values in their place, can miss the bound.
Values may be sent and summed in bfloat16 or wider, within the bound.
No kernel may reach another device: no remote copies, remote signals or barrier semaphores. Data moves between devices by JAX's collectives and lax.ppermute only.
A program may use at most 128 MiB of HBM per device.

```python
import jax
import jax.numpy as jnp
from jax import lax

D = 1024
H = 16
DH = 64
CROWS = 512
SLOT = 128
QUERIES = 8
VARIATES = 8
BPQ = 1
DOC_DEV = 1024
DOCS_DEV = 16
BLOCKS = 8
CACHE_ROWS = 4096
DOC_TOK = 8192
DOCS = 128


def document_plan(key):
    plan_key = jax.random.fold_in(key, 101)
    cut_key, order_key = jax.random.split(plan_key)
    device_count = DOC_TOK // DOC_DEV
    cut_points = jax.random.randint(cut_key, (device_count, QUERIES), SLOT // 4, SLOT - SLOT // 4 + 1)
    order_keys = jax.random.split(order_key, device_count)
    slot_orders = jax.vmap(lambda one_key: jax.random.permutation(one_key, QUERIES))(order_keys)
    return (cut_points, slot_orders)


def draw_doc_seg(key, part):
    cut_points, slot_orders = document_plan(key)
    device_count = DOC_TOK // DOC_DEV
    offset = jnp.arange(SLOT, dtype=jnp.int32)
    second = (offset[None, None, :] >= cut_points[:, :, None]).astype(jnp.int32)
    slot_ids = 2 * jnp.arange(QUERIES, dtype=jnp.int32)[None, :, None]
    device_ids = DOCS_DEV * jnp.arange(device_count, dtype=jnp.int32)[:, None, None]
    return (device_ids + slot_ids + second).reshape(DOC_TOK).astype(jnp.int32)


def draw_doc_query(key, part):
    cut_points, slot_orders = document_plan(key)
    return jnp.repeat(slot_orders, 2, axis=1).reshape(DOCS).astype(jnp.int32)


def draw_query_len(key, part):
    drawn = jax.random.randint(key, (QUERIES,), CROWS // 2, BPQ * CROWS + 1)
    return drawn.at[0].set(BPQ * CROWS).astype(jnp.int32)


def draw_cache_k(key, part):
    first_key = jax.random.fold_in(jax.random.fold_in(key, 11), 0)
    values = jnp.clip(jax.random.normal(first_key, (CACHE_ROWS, D), jnp.float32) * 2.5, -15.0, 15.0)
    return values.astype(jnp.bfloat16)


def with_ends(values, own_key, smallest, largest):
    index_at = [jax.random.randint(jax.random.fold_in(own_key, axis), (), 0, length) for axis, length in enumerate(values.shape)]
    main_axis = values.shape.index(max(values.shape))
    neighbour = index_at[:main_axis] + [(index_at[main_axis] + 1) % values.shape[main_axis]] + index_at[main_axis + 1:]
    return values.at[tuple(index_at)].set(smallest).at[tuple(neighbour)].set(largest)


def steps_of(own_key, dims, cuts, low, largest):
    def one(axis_at, shards_of):
        steps = jax.random.uniform(jax.random.fold_in(jax.random.fold_in(own_key, 6), axis_at), (shards_of,), jnp.float32, low / len(cuts), largest / len(cuts))
        return jnp.repeat(jnp.exp(steps), dims[axis_at] // shards_of).reshape((-1,) + (1,) * (len(dims) - axis_at - 1))

    loudness = one(*cuts[0])
    for cut in cuts[1:]:
        loudness = loudness * one(*cut)
    return loudness


def scatter_about(key, shape, spread, reach, pieces=(), kind=jnp.bfloat16):
    level = steps_of(key, shape, pieces, -0.22, 0.18) if pieces else 1.0
    values = jax.random.normal(key, shape, jnp.float32) * spread * level
    return jnp.minimum(jnp.maximum(values, -reach), reach).astype(kind)


def setup_inputs(seed: int = 0) -> dict:
    seeds = jax.random.split(jax.random.key(seed), 17)
    doc_x = scatter_about(seeds[0], (DOC_TOK, D), 1.0, 6.0, ((0, 8),))
    doc_seg = draw_doc_seg(jax.random.fold_in(seeds[16], 71), 0)
    doc_query = draw_doc_query(jax.random.fold_in(seeds[16], 71), 0)
    doc_var = with_ends(jax.random.randint(seeds[3], (DOC_TOK,), 0, VARIATES), jax.random.fold_in(seeds[3], 1), 0, VARIATES - 1).astype(jnp.int32)
    query_len = draw_query_len(jax.random.fold_in(seeds[16], 71), 0)
    block_perm = jax.random.permutation(seeds[5], BLOCKS).astype(jnp.int32)
    cache_k = draw_cache_k(jax.random.fold_in(seeds[16], 71), 0)
    cache_v = scatter_about(seeds[7], (CACHE_ROWS, D), 1.0, 6.0, ((0, 8), (1, 4)))
    cache_var = with_ends(jax.random.randint(seeds[8], (CACHE_ROWS,), 0, VARIATES), jax.random.fold_in(seeds[8], 1), 0, VARIATES - 1).astype(jnp.int32)
    w_query = scatter_about(seeds[9], (D, D), D ** -0.5, 0.1875, ((1, 4),))
    w_key = scatter_about(seeds[10], (D, D), (D // 9) ** -0.5, 0.5, ((1, 4),))
    w_value = scatter_about(seeds[11], (D, D), D ** -0.5, 0.1875, ((1, 4),))
    w_out = scatter_about(seeds[12], (D, D), D ** -0.5, 0.1875, ((0, 4),))
    var_bias = jnp.clip(jax.random.uniform(seeds[13], (2, H), jnp.float32, -1.0, 1.0) * steps_of(seeds[13], (2, H), ((1, 4),), -0.4, 0.0), -1.0, 1.0)
    norm_gain = jnp.clip(1.0 + 0.18 * jax.random.normal(seeds[14], (D,), jnp.float32), 0.1, 1.9)
    readout = scatter_about(seeds[15], (D,), (D // 64) ** -0.5, 1.5, (), jnp.float32)
    return {"doc_x": doc_x, "doc_seg": doc_seg, "doc_query": doc_query, "doc_var": doc_var, "query_len": query_len, "block_perm": block_perm, "cache_k": cache_k, "cache_v": cache_v, "cache_var": cache_var, "w_query": w_query, "w_key": w_key, "w_value": w_value, "w_out": w_out, "var_bias": var_bias, "norm_gain": norm_gain, "readout": readout}


def rotary(projected, positions):
    row_count = projected.shape[0]
    head_count = projected.shape[1] // DH
    half_size = DH // 2
    shaped = projected.reshape(row_count, head_count, DH)
    frequency = 10000.0 ** (-jnp.arange(half_size, dtype=jnp.float32) / half_size)
    angles = positions.astype(jnp.float32)[:, None] * frequency[None, :]
    cosine = jnp.cos(angles)[:, None, :]
    sine_part = jnp.sin(angles)[:, None, :]
    first_half = shaped[:, :, :half_size]
    second_half = shaped[:, :, half_size:]
    turned = jnp.concatenate([first_half * cosine - second_half * sine_part, second_half * cosine + first_half * sine_part], axis=2)
    return turned.reshape(row_count, head_count * DH)

def softmax_part(scores, allowed):
    scores = jnp.where(allowed, scores, -1e+30)
    peak = lax.optimization_barrier(jnp.max(scores, axis=-1))
    weights = jnp.where(allowed, jnp.exp(scores - peak[..., None]), 0.0)
    return (peak, lax.optimization_barrier(jnp.sum(weights, axis=-1)), weights.astype(jnp.bfloat16))

def reference(doc_x, doc_seg, doc_query, doc_var, query_len, block_perm, cache_k, cache_v, cache_var, w_query, w_key, w_value, w_out, var_bias, norm_gain, readout):
    token_count = doc_x.shape[0]
    doc_count = doc_query.shape[0]
    lengths = jax.ops.segment_sum(jnp.ones((token_count,), jnp.int32), doc_seg, num_segments=doc_count).astype(jnp.int32)
    starts = (jnp.cumsum(lengths) - lengths).astype(jnp.int32)
    tok_query = doc_query[doc_seg].astype(jnp.int32)
    positions = (query_len[tok_query] + jnp.arange(token_count, dtype=jnp.int32) - starts[doc_seg]).astype(jnp.int32)
    query_rot = rotary(jnp.dot(doc_x, w_query, preferred_element_type=jnp.float32), positions).astype(jnp.bfloat16)
    key_rot = rotary(jnp.dot(doc_x, w_key, preferred_element_type=jnp.float32), positions).astype(jnp.bfloat16)
    value_proj = jnp.dot(doc_x, w_value, preferred_element_type=jnp.float32).astype(jnp.bfloat16)

    def heads_first(array):
        return array.reshape(array.shape[0], H, DH).transpose(1, 0, 2)
    slot_total = token_count // SLOT
    seg_slots = doc_seg.reshape(slot_total, SLOT)
    var_slots = doc_var.reshape(slot_total, SLOT)
    self_allowed = seg_slots[:, :, None] == seg_slots[:, None, :]
    var_equal = var_slots[:, :, None] == var_slots[:, None, :]

    def self_head(head_inputs):
        head_q, head_k, head_v, bias_pair = head_inputs
        slot_q = head_q.reshape(slot_total, SLOT, DH).astype(jnp.float32)
        slot_k = head_k.reshape(slot_total, SLOT, DH).astype(jnp.float32)
        slot_v = head_v.reshape(slot_total, SLOT, DH).astype(jnp.float32)
        scores = jnp.einsum('gtd,gsd->gts', slot_q, slot_k) * 0.125
        scores = scores + jnp.where(var_equal, bias_pair[0], bias_pair[1])
        peak, total_weight, weights = softmax_part(scores, self_allowed)
        sums = jnp.einsum('gts,gsd->gtd', weights.astype(jnp.float32), slot_v)
        return (peak.reshape(token_count), total_weight.reshape(token_count), sums.reshape(token_count, DH))
    self_peak, self_total, self_sum = lax.map(self_head, (heads_first(query_rot), heads_first(key_rot), heads_first(value_proj), var_bias.T))
    token_order = jnp.argsort(tok_query, stable=True).astype(jnp.int32)
    restore = jnp.argsort(token_order).astype(jnp.int32)
    per_query = token_count // QUERIES
    holder = jnp.argsort(block_perm).astype(jnp.int32)
    query_rows = BPQ * CROWS
    query_keys = cache_k.reshape(BLOCKS, CROWS, D)[holder].reshape(QUERIES, query_rows, H, DH)
    query_values = cache_v.reshape(BLOCKS, CROWS, D)[holder].reshape(QUERIES, query_rows, H, DH)
    query_cvar = cache_var.reshape(BLOCKS, CROWS)[holder].reshape(QUERIES, query_rows)
    row_valid = jnp.arange(query_rows, dtype=jnp.int32)[None, :] < query_len[:, None]
    sorted_q = query_rot[token_order].reshape(QUERIES, per_query, H, DH)
    sorted_var = doc_var[token_order].reshape(QUERIES, per_query)
    block_size = 512 if per_query % 512 == 0 else per_query
    block_count = per_query // block_size

    def one_query(query_inputs):
        keys, values, cvar, valid, tok_q, tok_var = query_inputs

        def one_head(head_inputs):
            head_k, head_v, head_q, bias_pair = head_inputs

            def one_block(block_inputs):
                block_q, block_var = block_inputs
                scores = jnp.dot(block_q, head_k.T, preferred_element_type=jnp.float32) * 0.125
                scores = scores + jnp.where(block_var[:, None] == cvar[None, :], bias_pair[0], bias_pair[1])
                allowed = jnp.broadcast_to(valid[None, :], scores.shape)
                peak, total_weight, weights = softmax_part(scores, allowed)
                return (peak, total_weight, jnp.dot(weights, head_v, preferred_element_type=jnp.float32))
            peaks, totals, sums = lax.map(one_block, (head_q.reshape(block_count, block_size, DH), tok_var.reshape(block_count, block_size)))
            return (peaks.reshape(per_query), totals.reshape(per_query), sums.reshape(per_query, DH))
        return lax.map(one_head, (keys.transpose(1, 0, 2), values.transpose(1, 0, 2), tok_q.transpose(1, 0, 2), var_bias.T))
    cache_peak, cache_total, cache_sum = lax.map(one_query, (query_keys, query_values, query_cvar, row_valid, sorted_q, sorted_var))
    cache_peak = cache_peak.transpose(1, 0, 2).reshape(H, token_count)[:, restore]
    cache_total = cache_total.transpose(1, 0, 2).reshape(H, token_count)[:, restore]
    cache_sum = cache_sum.transpose(1, 0, 2, 3).reshape(H, token_count, DH)[:, restore]
    peak = jnp.maximum(cache_peak, self_peak)
    cache_factor = jnp.exp(cache_peak - peak)
    self_factor = jnp.exp(self_peak - peak)
    numerator = cache_sum * cache_factor[..., None] + self_sum * self_factor[..., None]
    denominator = cache_total * cache_factor + self_total * self_factor
    attended = (numerator / denominator[..., None]).transpose(1, 0, 2).reshape(token_count, H * DH).astype(jnp.bfloat16)
    update_sum = jnp.dot(attended, w_out, preferred_element_type=jnp.float32)
    hidden = doc_x.astype(jnp.float32) + update_sum
    square_sum = lax.optimization_barrier(jnp.sum(hidden * hidden, axis=1))
    weighted = lax.optimization_barrier(jnp.sum(hidden * norm_gain * readout, axis=1))
    token_score = weighted * lax.rsqrt(square_sum / D + 1e-06)
    pooled = jax.ops.segment_sum(token_score, doc_seg, num_segments=doc_count) / lengths.astype(jnp.float32)
    return (update_sum, pooled)
```

```python
import functools

import jax
import jax.numpy as jnp
import numpy as np
from jax import lax
from jax.experimental import pallas as pl
from jax.experimental.pallas import tpu as pltpu
from jax.sharding import PartitionSpec as P

DH = 64
QUERIES = 8
LANES = 128
EXTRA = 16
NEVER = -1e30
BF = jnp.bfloat16
F32 = jnp.float32
VMEM = pl.BlockSpec(memory_space=pltpu.VMEM)
SMEM = pl.BlockSpec(memory_space=pltpu.SMEM)
LIMIT = 32 * 1024 * 1024


def offset_tables(slot_rows):
    half = DH // 2
    freq = (10000.0 ** (-np.arange(half, dtype=np.float64) / half)).astype(np.float32)
    lane_freq = np.tile(freq, LANES // half)
    angles = np.arange(slot_rows, dtype=np.float64)[:, None] * lane_freq[None, :].astype(np.float64)
    sign = np.where(np.arange(LANES) % DH < half, -1.0, 1.0).astype(np.float32)
    rows = np.zeros((8, LANES), np.float32)
    rows[0] = lane_freq
    rows[1] = sign
    return np.cos(angles).astype(np.float32), np.sin(angles).astype(np.float32), rows


def dot(a, b):
    return jnp.dot(a, b, preferred_element_type=F32)


def dot_t(a, b):
    return lax.dot_general(a, b, (((1,), (1,)), ((), ())), preferred_element_type=F32)


def slot_of(p, doc_query, block_perm, slots, bpq):
    blk = lax.axis_index("blk")
    wanted = block_perm[blk ^ p] // bpq
    slot = jnp.int32(0)
    for j in range(slots):
        slot = slot + jnp.where(doc_query[blk * 2 * slots + 2 * j] == wanted, j, 0)
    return slot


def start_tables(doc_query, query_len, seg_ref, rows_ref, base_ref):
    slots, width = seg_ref.shape
    blk = lax.axis_index("blk")
    row = lax.broadcasted_iota(jnp.int32, (slots, width), 0)
    length = jnp.zeros((slots, width), F32)
    for j in range(slots):
        value = query_len[doc_query[blk * 2 * slots + 2 * j]].astype(F32)
        length = jnp.where(row == j, value, length)
    second = (seg_ref[...] & 1).astype(F32)
    count = width - jnp.sum(second, axis=1, keepdims=True)
    count = jnp.broadcast_to(count, (slots, width))
    freq = rows_ref[0:1, :]
    one, two = length * freq, (length - count) * freq
    base_ref[0] = jnp.cos(one)
    base_ref[1] = jnp.sin(one)
    base_ref[2] = jnp.cos(two)
    base_ref[3] = jnp.sin(two)
    base_ref[4] = count


def slot_tables(slot, base_ref, cos_ref, sin_ref, rows_ref):
    shape = cos_ref.shape
    rows = [base_ref[i, pl.ds(slot, 1), :] for i in range(5)]
    token = lax.broadcasted_iota(jnp.int32, shape, 0).astype(F32)
    first = token < rows[4]
    base_cos = jnp.where(first, rows[0], rows[2])
    base_sin = jnp.where(first, rows[1], rows[3])
    off_cos, off_sin = cos_ref[...], sin_ref[...]
    cos = base_cos * off_cos - base_sin * off_sin
    sin = (base_sin * off_cos + base_cos * off_sin) * rows_ref[1:2, :]
    return cos, sin


def turn(value, cos, sin):
    lane = lax.broadcasted_iota(jnp.int32, cos.shape, 1)
    low = lane % DH < DH // 2
    parts = []
    for at in range(0, value.shape[1], LANES):
        part = value[:, at : at + LANES]
        other = jnp.where(
            low, pltpu.roll(part, LANES - DH // 2, 1), pltpu.roll(part, DH // 2, 1)
        )
        parts.append(part * cos + other * sin)
    return jnp.concatenate(parts, axis=1)


def query_kernel(
    bpq, doc_query, query_len, block_perm, x_ref, w_ref, seg_ref, var_ref, cos_ref, sin_ref,
    rows_ref, *refs
):
    pick_ref, base_ref, y_ref = refs[0], refs[-2], refs[-1]
    q_refs = refs[1:-2]
    slots, width = seg_ref.shape
    start_tables(doc_query, query_len, seg_ref, rows_ref, base_ref)
    y_ref[...] = dot(x_ref[...], w_ref[...])
    for k, q_ref in enumerate(q_refs):
        for j in range(2):
            slot = slot_of(2 * k + j, doc_query, block_perm, slots, bpq)
            pick_ref[2 * k + j] = slot
            cos, sin = slot_tables(slot, base_ref, cos_ref, sin_ref, rows_ref)
            at = pl.ds(pl.multiple_of(slot * width, width), width)
            turned = turn(y_ref[at, :], cos, sin)
            q_ref[j * width : (j + 1) * width, :] = (turned * 0.125).astype(BF)
            var = var_ref[pl.ds(slot, 1), :].astype(F32)
            q_ref[2 * width :, j * width : (j + 1) * width] = jnp.broadcast_to(
                var, (EXTRA, width)
            ).astype(BF)


def pack_kernel(k_ref, v_ref, var_ref, out_ref):
    rows, cols = k_ref.shape
    out_ref[0:rows, :] = k_ref[...]
    for i in range(rows // cols):
        block = v_ref[i * cols : (i + 1) * cols, :].astype(F32)
        out_ref[rows + i * cols : rows + (i + 1) * cols, :] = block.T.astype(BF)
    parts = rows // LANES
    var = var_ref[...].astype(F32)
    var = jnp.concatenate([var, jnp.zeros((EXTRA - parts, LANES), F32)], axis=0)
    out_ref[2 * rows :, :] = jnp.concatenate([var, var], axis=1).astype(BF)


def by_head(query):
    lane = lax.broadcasted_iota(jnp.int32, query.shape, 1) // DH
    heads = query.shape[1] // DH
    return jnp.concatenate(
        [jnp.where(lane == h, query, jnp.zeros_like(query)) for h in range(heads)], axis=0
    )


def attend(scores, same, allowed, bias_ref, values, out_ref, at):
    width = same.shape[1]
    stats = []
    for h in range(scores.shape[1] // width):
        part = scores[:, h * width : (h + 1) * width]
        part = part + jnp.where(same, bias_ref[0, h], bias_ref[1, h])
        part = jnp.where(allowed, part, NEVER)
        peak = jnp.max(part, axis=0, keepdims=True)
        weight = jnp.exp(part - peak)
        total = jnp.sum(weight, axis=0, keepdims=True)
        weight = weight.astype(BF)
        mixed = None
        key = 0
        for value in values:
            keys = value.shape[1]
            term = dot(value[h * DH : (h + 1) * DH, :], weight[key : key + keys, :])
            mixed = term if mixed is None else mixed + term
            key += keys
        mixed = mixed * (1.0 / total)
        out_ref[h * DH : (h + 1) * DH, at] = mixed.astype(out_ref.dtype)
        stats.append(peak + jnp.log(total))
    return stats


def cache_kernel(bpq, query_len, block_perm, bias_ref, q_ref, own_ref, other_ref, out_ref):
    blk = lax.axis_index("blk")
    width = q_ref.shape[0] // 2 - EXTRA // 2
    cols = q_ref.shape[1]
    rows = (own_ref.shape[0] - EXTRA) // 2
    for j, ref in enumerate((own_ref, other_ref)):
        block = block_perm[blk ^ j]
        usable = query_len[block // bpq] - block % bpq * rows
        var = ref[2 * rows :, 0:LANES].astype(F32)
        var = jnp.concatenate([var, jnp.zeros((LANES - EXTRA, LANES), F32)], axis=0).T
        key_var = jnp.concatenate(
            [jnp.broadcast_to(var[:, i : i + 1], (LANES, width)) for i in range(rows // LANES)],
            axis=0,
        )
        tok_var = q_ref[2 * width :, j * width : (j + 1) * width].astype(F32)[0:1, :]
        same = key_var == tok_var
        allowed = lax.broadcasted_iota(jnp.int32, (rows, width), 0) < usable
        scores = dot_t(ref[0:rows, :], by_head(q_ref[j * width : (j + 1) * width, :]))
        values = [ref[rows + i * cols : rows + (i + 1) * cols, :] for i in range(rows // cols)]
        at = slice(j * width, (j + 1) * width)
        stats = attend(scores, same, allowed, bias_ref, values, out_ref, at)
        full = jnp.concatenate(stats, axis=0)
        high = full.astype(BF).astype(F32)
        middle = (full - high).astype(BF).astype(F32)
        low = full - high - middle
        pad = jnp.zeros((EXTRA - 3 * len(stats), width), F32)
        out_ref[cols:, at] = jnp.concatenate([high, middle, low, pad], axis=0).astype(BF)


def own_kernel(
    doc_query, query_len, bias_ref, home_ref, x_ref, wk_ref, wv_ref, seg_ref, var_ref, cos_ref,
    sin_ref, rows_ref, *refs
):
    out_ref, base_ref, k_ref, v_ref = refs[-4:]
    q_refs = refs[:-4]
    slots, width = seg_ref.shape
    cols = wk_ref.shape[1]
    start_tables(doc_query, query_len, seg_ref, rows_ref, base_ref)
    k_ref[...] = dot(x_ref[...], wk_ref[...])
    v_ref[...] = dot(x_ref[...], wv_ref[...])
    for n in range(slots):
        slot = home_ref[n]
        cos, sin = slot_tables(slot, base_ref, cos_ref, sin_ref, rows_ref)
        at = pl.ds(pl.multiple_of(slot * width, width), width)
        key = turn(k_ref[at, :], cos, sin).astype(BF)
        value = v_ref[at, :].T.astype(BF)
        query = q_refs[n // 2][n % 2 * width : (n % 2 + 1) * width, :]
        scores = dot_t(key, by_head(query))
        var = jnp.broadcast_to(var_ref[pl.ds(slot, 1), :].astype(F32), (width, width))
        same = var.T == var
        count = base_ref[4, pl.ds(slot, 1), :]
        key_second = lax.broadcasted_iota(jnp.int32, (width, width), 0).astype(F32) >= count
        tok_second = lax.broadcasted_iota(jnp.int32, (width, width), 1).astype(F32) >= count
        allowed = jnp.logical_not(jnp.logical_xor(key_second, tok_second))
        part_ref = out_ref.at[n]
        stats = attend(scores, same, allowed, bias_ref, [value], part_ref, slice(None))
        stats = jnp.concatenate(stats + [jnp.zeros((8 - len(stats), width), F32)], axis=0)
        part_ref[cols:, :] = stats


def merge_kernel(first, got_ref, own_ref, out_ref):
    cols = got_ref.shape[0] - EXTRA
    heads = cols // DH
    width = got_ref.shape[1] // 2
    for j in range(2):
        at = slice(j * width, (j + 1) * width)
        stats = got_ref[cols:, at].astype(F32)
        there = stats[0:heads] + stats[heads : 2 * heads] + stats[2 * heads : 3 * heads]
        here = own_ref[first + j, cols : cols + heads, :]
        peak = jnp.maximum(there, here)
        there, here = jnp.exp(there - peak), jnp.exp(here - peak)
        inverse = 1.0 / (there + here)
        there, here = there * inverse, here * inverse
        parts = []
        for h in range(heads):
            row = slice(h * DH, (h + 1) * DH)
            parts.append(
                got_ref[row, at].astype(F32) * there[h : h + 1]
                + own_ref[first + j, row, :] * here[h : h + 1]
            )
        out_ref[at, :] = jnp.concatenate(parts, axis=0).T.astype(BF)


def output_kernel(head_count, first, home_ref, *refs):
    att_refs, w_refs = refs[:head_count], refs[head_count : 2 * head_count]
    x_ref, seg_ref, gain_ref, read_ref = refs[2 * head_count : 2 * head_count + 4]
    update_ref, pooled_ref, sum_ref = refs[-3:]
    step = pl.program_id(0)
    slot = home_ref[first + step]
    total = dot(att_refs[0][...], w_refs[0][...])
    for att_ref, w_ref in zip(att_refs[1:], w_refs[1:]):
        total = total + dot(att_ref[...], w_ref[...])
    sum_ref[...] = total
    cols = update_ref.shape[1]
    head = lax.axis_index("head")
    update_ref[...] = sum_ref[:, pl.ds(pl.multiple_of(head * cols, cols), cols)]
    hidden = x_ref[...].astype(F32) + total
    square = jnp.sum(hidden * hidden, axis=1, keepdims=True)
    weighted = jnp.sum(hidden * (gain_ref[...] * read_ref[...]), axis=1, keepdims=True)
    score = weighted * lax.rsqrt(square / hidden.shape[1] + 1e-06)
    width = score.shape[0]
    second = (seg_ref[pl.ds(slot, 1), :] & 1).astype(F32)
    count_two = jnp.sum(second, axis=1, keepdims=True)
    count_one = width - count_two
    token = lax.broadcasted_iota(jnp.int32, score.shape, 0).astype(F32)
    is_first = token < count_one
    sum_one = jnp.sum(jnp.where(is_first, score, 0.0), axis=0, keepdims=True)
    sum_two = jnp.sum(jnp.where(is_first, 0.0, score), axis=0, keepdims=True)
    lane = lax.broadcasted_iota(jnp.int32, (1, LANES), 1)
    pooled_ref[0] = jnp.where(lane == 0, sum_one / count_one, sum_two / count_two)


def call(kernel, out, ins, scratch=(), flops=0, bytes_accessed=0, **kwargs):
    return pl.pallas_call(
        kernel,
        out_shape=out,
        in_specs=ins,
        scratch_shapes=list(scratch),
        compiler_params=pltpu.CompilerParams(vmem_limit_bytes=LIMIT),
        cost_estimate=pl.CostEstimate(
            flops=flops, bytes_accessed=bytes_accessed, transcendentals=0
        ),
        **kwargs,
    )


def partner(value, axis, k):
    count = lax.axis_size(axis)
    return lax.ppermute(value, axis, [(i, i ^ k) for i in range(count)])


def spread_merge(backs, own, pick, slots, bpq):
    cols = backs[0].shape[0] - EXTRA
    width = backs[0].shape[1] // 2
    heads = cols // DH
    parts = jnp.stack(backs).reshape(len(backs), cols + EXTRA, 2, width)
    parts = parts.transpose(0, 2, 1, 3).reshape(2 * len(backs), cols + EXTRA, width)
    order = jnp.argsort(pick, stable=True)
    parts = jnp.take(parts, order, axis=0).reshape(slots, bpq, cols + EXTRA, width)
    stats = parts[:, :, cols : cols + 3 * heads].astype(F32)
    stats = stats.reshape(slots, bpq, 3, heads, width).sum(axis=2)
    stats = jnp.concatenate([stats, own[:, None, cols : cols + heads]], axis=1)
    weight = jnp.exp(stats - jnp.max(stats, axis=1, keepdims=True))
    weight = weight / jnp.sum(weight, axis=1, keepdims=True)
    values = jnp.concatenate([parts[:, :, :cols].astype(F32), own[:, None, :cols]], axis=1)
    values = values.reshape(slots, bpq + 1, heads, DH, width)
    mixed = jnp.sum(values * weight[:, :, :, None, :], axis=1).reshape(slots, cols, width)
    mixed = mixed.transpose(0, 2, 1).astype(BF)
    return [mixed[2 * k : 2 * k + 2].reshape(2 * width, cols) for k in range(slots // 2)]


def body(
    doc_x, doc_seg, doc_query, doc_var, query_len, block_perm, cache_k, cache_v, cache_var,
    w_query, w_key, w_value, w_out, var_bias, norm_gain, readout,
):
    rows, depth = doc_x.shape
    cols = w_query.shape[1]
    blocks = lax.axis_size("blk")
    head_count = lax.axis_size("head")
    bpq = blocks // QUERIES
    slots = QUERIES
    width = rows // slots
    chunks = blocks // 2
    cache_rows = cache_k.shape[0]
    seg = doc_seg.reshape(slots, width)
    var = doc_var.reshape(slots, width)
    cos, sin, freq_rows = offset_tables(width)
    sds = jax.ShapeDtypeStruct
    chunk_shape = sds((2 * width + EXTRA, cols), BF)
    base = pltpu.VMEM((5, slots, width), F32)

    w_parts = [w_out] + [partner(w_out, "head", r) for r in range(1, head_count)]

    pick, *queries = call(
        functools.partial(query_kernel, bpq),
        [sds((blocks,), jnp.int32)] + [chunk_shape] * chunks,
        [SMEM] * 3 + [VMEM] * 7,
        [base, pltpu.VMEM((rows, cols), F32)],
        flops=2 * rows * depth * cols,
        bytes_accessed=2 * rows * depth,
        out_specs=[SMEM] + [VMEM] * chunks,
        name="query",
    )(doc_query, query_len, block_perm, doc_x, w_query, seg, var, cos, sin, freq_rows)

    asked = [queries[0]] + [partner(queries[k], "blk", 2 * k) for k in range(1, chunks)]

    packed = call(
        pack_kernel,
        sds((2 * cache_rows + EXTRA, cols), BF),
        [VMEM] * 3,
        bytes_accessed=8 * cache_rows * cols,
        out_specs=VMEM,
        name="pack",
    )(cache_k, cache_v, cache_var.reshape(cache_rows // LANES, LANES))
    packed_other = partner(packed, "blk", 1)

    if bpq == 1:
        home = pick
        home_queries = queries
    else:
        home = jnp.arange(slots, dtype=jnp.int32)
        every = jnp.stack([q[: 2 * width] for q in queries]).reshape(blocks, width, cols)
        every = jnp.take(every, jnp.argsort(pick, stable=True)[::bpq], axis=0)
        home_queries = [
            every[2 * k : 2 * k + 2].reshape(2 * width, cols) for k in range(slots // 2)
        ]

    own = call(
        own_kernel,
        sds((slots, cols + 8, width), F32),
        [SMEM] * 4 + [VMEM] * (8 + len(home_queries)),
        [base, pltpu.VMEM((rows, cols), F32), pltpu.VMEM((rows, cols), F32)],
        flops=6 * rows * depth * cols,
        bytes_accessed=2 * rows * depth,
        out_specs=VMEM,
        name="own_documents",
    )(
        doc_query, query_len, var_bias, home, doc_x, w_key, w_value, seg, var, cos, sin,
        freq_rows, *home_queries,
    )

    def from_cache(query):
        return call(
            functools.partial(cache_kernel, bpq),
            chunk_shape,
            [SMEM] * 3 + [VMEM] * 3,
            flops=16 * width * cache_rows * cols,
            bytes_accessed=8 * cache_rows * cols,
            out_specs=VMEM,
            name="cache_part",
        )(query_len, block_perm, var_bias, query, packed, packed_other)

    parts = [from_cache(query) for query in asked]
    backs = [parts[0]] + [partner(parts[k], "blk", 2 * k) for k in range(1, chunks)]

    if bpq == 1:
        attended = [
            call(
                functools.partial(merge_kernel, 2 * k),
                sds((2 * width, cols), BF),
                [VMEM] * 2,
                bytes_accessed=4 * rows * cols,
                out_specs=VMEM,
                name="merge",
            )(backs[k], own)
            for k in range(chunks)
        ]
    else:
        attended = spread_merge(backs, own, pick, slots, bpq)

    gain, read = norm_gain.reshape(1, depth), readout.reshape(1, depth)
    update = pooled = None
    for k in range(slots // 2):
        atts = [attended[k]] + [partner(attended[k], "head", r) for r in range(1, head_count)]
        chained = [] if update is None else [update, pooled]
        arguments = atts + w_parts + [doc_x, seg, gain, read]
        whole = lambda i, home: (0, 0)
        at_slot = functools.partial(lambda k, i, home: (home[2 * k + i], 0), k)
        update, pooled = pl.pallas_call(
            functools.partial(output_kernel, head_count, 2 * k),
            out_shape=[sds((rows, cols), F32), sds((slots, 1, LANES), F32)],
            grid_spec=pltpu.PrefetchScalarGridSpec(
                num_scalar_prefetch=1,
                grid=(2,),
                in_specs=[pl.BlockSpec((width, cols), lambda i, home: (i, 0))] * head_count
                + [pl.BlockSpec((cols, depth), whole)] * head_count
                + [
                    pl.BlockSpec((width, depth), at_slot),
                    pl.BlockSpec((slots, width), whole),
                    pl.BlockSpec((1, depth), whole),
                    pl.BlockSpec((1, depth), whole),
                ]
                + [pl.BlockSpec(memory_space=pl.ANY)] * len(chained),
                out_specs=[
                    pl.BlockSpec((width, cols), at_slot),
                    pl.BlockSpec(
                        (1, 1, LANES),
                        functools.partial(lambda k, i, home: (home[2 * k + i], 0, 0), k),
                    ),
                ],
                scratch_shapes=[pltpu.VMEM((width, depth), F32)],
            ),
            input_output_aliases=(
                {1 + len(arguments): 0, 2 + len(arguments): 1} if chained else {}
            ),
            compiler_params=pltpu.CompilerParams(vmem_limit_bytes=LIMIT),
            cost_estimate=pl.CostEstimate(
                flops=4 * width * depth * depth,
                bytes_accessed=2 * depth * depth,
                transcendentals=0,
            ),
            name="output",
        )(home, *arguments, *chained)
    return (update, pooled[:, 0, :2].reshape(2 * slots))


def solution(mesh):
    return jax.shard_map(
        body,
        mesh=mesh,
        in_specs=(
            P("blk", None), P("blk"), P(), P("blk"), P(), P(), P("blk", "head"),
            P("blk", "head"), P("blk"), P(None, "head"), P(None, "head"), P(None, "head"),
            P("head", None), P(None, "head"), P(), P(),
        ),
        out_specs=(P("blk", "head"), P("blk")),
        check_vma=False,
    )
```

```python
import functools

import jax
import jax.numpy as jnp
import numpy as np
from jax import lax
from jax.experimental import pallas as pl
from jax.experimental.pallas import tpu as pltpu
from jax.sharding import PartitionSpec as P

DH = 64
QUERIES = 8
LANES = 128
EXTRA = 16
NEVER = -1e30
BF = jnp.bfloat16
F32 = jnp.float32
VMEM = pl.BlockSpec(memory_space=pltpu.VMEM)
SMEM = pl.BlockSpec(memory_space=pltpu.SMEM)
HBM = pl.BlockSpec(memory_space=pltpu.HBM)
ANY = pl.BlockSpec(memory_space=pl.ANY)
DMA = pltpu.SemaphoreType.DMA
LIMIT = 32 * 1024 * 1024


def offset_tables(slot_rows):
    half = DH // 2
    freq = (10000.0 ** (-np.arange(half, dtype=np.float64) / half)).astype(np.float32)
    lane_freq = np.tile(freq, LANES // half)
    angles = np.arange(slot_rows, dtype=np.float64)[:, None] * lane_freq[None, :].astype(np.float64)
    sign = np.where(np.arange(LANES) % DH < half, -1.0, 1.0).astype(np.float32)
    rows = np.zeros((8, LANES), np.float32)
    rows[0] = lane_freq
    rows[1] = sign
    return np.cos(angles).astype(np.float32), np.sin(angles).astype(np.float32), rows


def dot(a, b):
    return jnp.dot(a, b, preferred_element_type=F32)


def dot_t(a, b):
    return lax.dot_general(a, b, (((1,), (1,)), ((), ())), preferred_element_type=F32)


def slot_of(p, doc_query, block_perm, slots, bpq):
    blk = lax.axis_index("blk")
    wanted = block_perm[blk ^ p] // bpq
    slot = jnp.int32(0)
    for j in range(slots):
        slot = slot + jnp.where(doc_query[blk * 2 * slots + 2 * j] == wanted, j, 0)
    return slot


def start_tables(doc_query, query_len, seg_ref, rows_ref, base_ref):
    slots, width = seg_ref.shape
    blk = lax.axis_index("blk")
    row = lax.broadcasted_iota(jnp.int32, (slots, width), 0)
    length = jnp.zeros((slots, width), F32)
    for j in range(slots):
        value = query_len[doc_query[blk * 2 * slots + 2 * j]].astype(F32)
        length = jnp.where(row == j, value, length)
    second = (seg_ref[...] & 1).astype(F32)
    count = width - jnp.sum(second, axis=1, keepdims=True)
    count = jnp.broadcast_to(count, (slots, width))
    freq = rows_ref[0:1, :]
    one, two = length * freq, (length - count) * freq
    base_ref[0] = jnp.cos(one)
    base_ref[1] = jnp.sin(one)
    base_ref[2] = jnp.cos(two)
    base_ref[3] = jnp.sin(two)
    base_ref[4] = count


def slot_tables(slot, base_ref, cos_ref, sin_ref, rows_ref):
    shape = cos_ref.shape
    rows = [base_ref[i, pl.ds(slot, 1), :] for i in range(5)]
    token = lax.broadcasted_iota(jnp.int32, shape, 0).astype(F32)
    first = token < rows[4]
    base_cos = jnp.where(first, rows[0], rows[2])
    base_sin = jnp.where(first, rows[1], rows[3])
    off_cos, off_sin = cos_ref[...], sin_ref[...]
    cos = base_cos * off_cos - base_sin * off_sin
    sin = (base_sin * off_cos + base_cos * off_sin) * rows_ref[1:2, :]
    return cos, sin


def turn(value, cos, sin):
    lane = lax.broadcasted_iota(jnp.int32, cos.shape, 1)
    low = lane % DH < DH // 2
    parts = []
    for at in range(0, value.shape[1], LANES):
        part = value[:, at : at + LANES]
        other = jnp.where(
            low, pltpu.roll(part, LANES - DH // 2, 1), pltpu.roll(part, DH // 2, 1)
        )
        parts.append(part * cos + other * sin)
    return jnp.concatenate(parts, axis=1)


def copies(sources, targets, sems):
    moves = [
        pltpu.make_async_copy(source, target, sems.at[i])
        for i, (source, target) in enumerate(zip(sources, targets))
    ]
    for move in moves:
        move.start()
    return moves


def query_kernel(bpq, chunks, *refs):
    sources = refs[:8]
    pick_ref, q_refs = refs[8], refs[9 : 9 + chunks]
    targets = refs[9 + chunks : 17 + chunks]
    base_ref, y_ref, sems = refs[17 + chunks :]
    moves = copies(sources, targets, sems)
    doc_query, query_len, block_perm, seg_ref, var_ref, table_ref, x_ref, w_ref = targets
    slots, width = seg_ref.shape
    cos_ref, sin_ref = table_ref.at[0:width], table_ref.at[width : 2 * width]
    rows_ref = table_ref.at[2 * width :]
    for move in moves[:6]:
        move.wait()
    start_tables(doc_query, query_len, seg_ref, rows_ref, base_ref)
    for move in moves[6:]:
        move.wait()
    y_ref[...] = dot(x_ref[...], w_ref[...])
    for k, q_ref in enumerate(q_refs):
        for j in range(2):
            slot = slot_of(2 * k + j, doc_query, block_perm, slots, bpq)
            pick_ref[2 * k + j] = slot
            cos, sin = slot_tables(slot, base_ref, cos_ref, sin_ref, rows_ref)
            at = pl.ds(pl.multiple_of(slot * width, width), width)
            turned = turn(y_ref[at, :], cos, sin)
            q_ref[j * width : (j + 1) * width, :] = (turned * 0.125).astype(BF)
            var = var_ref[pl.ds(slot, 1), :].astype(F32)
            q_ref[2 * width :, j * width : (j + 1) * width] = jnp.broadcast_to(
                var, (EXTRA, width)
            ).astype(BF)


def pack_kernel(k_hbm, v_hbm, var_hbm, w_hbm, after, out_ref, w_ref, v_ref, var_ref, sems):
    del after
    rows, cols = v_ref.shape
    moves = copies(
        [v_hbm, var_hbm, k_hbm, w_hbm], [v_ref, var_ref, out_ref.at[0:rows], w_ref], sems
    )
    moves[0].wait()
    for i in range(rows // cols):
        block = v_ref[i * cols : (i + 1) * cols, :].astype(F32)
        out_ref[rows + i * cols : rows + (i + 1) * cols, :] = block.T.astype(BF)
    moves[1].wait()
    parts = rows // LANES
    var = var_ref[...].astype(F32)
    var = jnp.concatenate([var, jnp.zeros((EXTRA - parts, LANES), F32)], axis=0)
    out_ref[2 * rows :, :] = jnp.concatenate([var, var], axis=1).astype(BF)
    for move in moves[2:]:
        move.wait()


def by_head(query):
    lane = lax.broadcasted_iota(jnp.int32, query.shape, 1) // DH
    heads = query.shape[1] // DH
    return jnp.concatenate(
        [jnp.where(lane == h, query, jnp.zeros_like(query)) for h in range(heads)], axis=0
    )


def attend(scores, same, allowed, bias_ref, values, out_ref, at):
    width = same.shape[1]
    stats = []
    for h in range(scores.shape[1] // width):
        part = scores[:, h * width : (h + 1) * width]
        part = part + jnp.where(same, bias_ref[0, h], bias_ref[1, h])
        part = jnp.where(allowed, part, NEVER)
        peak = jnp.max(part, axis=0, keepdims=True)
        weight = jnp.exp(part - peak)
        total = jnp.sum(weight, axis=0, keepdims=True)
        weight = weight.astype(BF)
        mixed = None
        key = 0
        for value in values:
            keys = value.shape[1]
            term = dot(value[h * DH : (h + 1) * DH, :], weight[key : key + keys, :])
            mixed = term if mixed is None else mixed + term
            key += keys
        mixed = mixed * (1.0 / total)
        out_ref[h * DH : (h + 1) * DH, at] = mixed.astype(out_ref.dtype)
        stats.append(peak + jnp.log(total))
    return stats


def cache_kernel(
    bpq, query_len, block_perm, bias_ref, q_ref, own_ref, other_ref, after, out_ref
):
    del after
    blk = lax.axis_index("blk")
    width = q_ref.shape[0] // 2 - EXTRA // 2
    cols = q_ref.shape[1]
    rows = (own_ref.shape[0] - EXTRA) // 2
    for j, ref in enumerate((own_ref, other_ref)):
        block = block_perm[blk ^ j]
        usable = query_len[block // bpq] - block % bpq * rows
        var = ref[2 * rows :, 0:LANES].astype(F32)
        var = jnp.concatenate([var, jnp.zeros((LANES - EXTRA, LANES), F32)], axis=0).T
        key_var = jnp.concatenate(
            [jnp.broadcast_to(var[:, i : i + 1], (LANES, width)) for i in range(rows // LANES)],
            axis=0,
        )
        tok_var = q_ref[2 * width :, j * width : (j + 1) * width].astype(F32)[0:1, :]
        same = key_var == tok_var
        allowed = lax.broadcasted_iota(jnp.int32, (rows, width), 0) < usable
        scores = dot_t(ref[0:rows, :], by_head(q_ref[j * width : (j + 1) * width, :]))
        values = [ref[rows + i * cols : rows + (i + 1) * cols, :] for i in range(rows // cols)]
        at = slice(j * width, (j + 1) * width)
        stats = attend(scores, same, allowed, bias_ref, values, out_ref, at)
        full = jnp.concatenate(stats, axis=0)
        high = full.astype(BF).astype(F32)
        middle = (full - high).astype(BF).astype(F32)
        low = full - high - middle
        pad = jnp.zeros((EXTRA - 3 * len(stats), width), F32)
        out_ref[cols:, at] = jnp.concatenate([high, middle, low, pad], axis=0).astype(BF)


def own_kernel(
    doc_query, query_len, bias_ref, home_ref, x_ref, wk_ref, wv_ref, seg_ref, var_ref, table_ref,
    after, *refs
):
    del after
    out_ref, base_ref, k_ref, v_ref = refs[-4:]
    q_refs = refs[:-4]
    slots, width = seg_ref.shape
    cols = wk_ref.shape[1]
    cos_ref, sin_ref = table_ref.at[0:width], table_ref.at[width : 2 * width]
    rows_ref = table_ref.at[2 * width :]
    start_tables(doc_query, query_len, seg_ref, rows_ref, base_ref)
    k_ref[...] = dot(x_ref[...], wk_ref[...])
    v_ref[...] = dot(x_ref[...], wv_ref[...])
    for n in range(slots):
        slot = home_ref[n]
        cos, sin = slot_tables(slot, base_ref, cos_ref, sin_ref, rows_ref)
        at = pl.ds(pl.multiple_of(slot * width, width), width)
        key = turn(k_ref[at, :], cos, sin).astype(BF)
        value = v_ref[at, :].T.astype(BF)
        query = q_refs[n // 2][n % 2 * width : (n % 2 + 1) * width, :]
        scores = dot_t(key, by_head(query))
        var = jnp.broadcast_to(var_ref[pl.ds(slot, 1), :].astype(F32), (width, width))
        same = var.T == var
        count = base_ref[4, pl.ds(slot, 1), :]
        key_second = lax.broadcasted_iota(jnp.int32, (width, width), 0).astype(F32) >= count
        tok_second = lax.broadcasted_iota(jnp.int32, (width, width), 1).astype(F32) >= count
        allowed = jnp.logical_not(jnp.logical_xor(key_second, tok_second))
        part_ref = out_ref.at[n]
        stats = attend(scores, same, allowed, bias_ref, [value], part_ref, slice(None))
        stats = jnp.concatenate(stats + [jnp.zeros((8 - len(stats), width), F32)], axis=0)
        part_ref[cols:, :] = stats


def merge_kernel(firsts, *refs):
    own_ref, out_ref = refs[-2:]
    for i, (first, got_ref) in enumerate(zip(firsts, refs)):
        cols = got_ref.shape[0] - EXTRA
        heads = cols // DH
        width = got_ref.shape[1] // 2
        for j in range(2):
            at = slice(j * width, (j + 1) * width)
            stats = got_ref[cols:, at].astype(F32)
            there = stats[0:heads] + stats[heads : 2 * heads] + stats[2 * heads : 3 * heads]
            here = own_ref[first + j, cols : cols + heads, :]
            peak = jnp.maximum(there, here)
            there, here = jnp.exp(there - peak), jnp.exp(here - peak)
            inverse = 1.0 / (there + here)
            there, here = there * inverse, here * inverse
            parts = []
            for h in range(heads):
                row = slice(h * DH, (h + 1) * DH)
                parts.append(
                    got_ref[row, at].astype(F32) * there[h : h + 1]
                    + own_ref[first + j, row, :] * here[h : h + 1]
                )
            to = slice((2 * i + j) * width, (2 * i + j + 1) * width)
            out_ref[to, :] = jnp.concatenate(parts, axis=0).T.astype(BF)


def output_kernel(head_count, firsts, last, home_ref, *refs):
    att_refs, w_refs = refs[:head_count], refs[head_count : 2 * head_count]
    x_hbm, seg_ref, gain_ref, read_ref = refs[2 * head_count : 2 * head_count + 4]
    before = refs[2 * head_count + 4 : -7]
    update_hbm, pooled_ref, x_ref, gr_ref, out_ref, in_sems, out_sems = refs[-7:]
    tokens, cols = att_refs[0].shape
    depth = w_refs[0].shape[1]
    width = tokens // (2 * len(firsts))
    places = [first + j for first in firsts for j in range(2)]
    found = [home_ref[place] for place in places]
    slots = [pl.ds(pl.multiple_of(slot * width, width), width) for slot in found]
    here = [slice(i * width, (i + 1) * width) for i in range(len(places))]
    reads = copies([x_hbm.at[at] for at in slots], [x_ref.at[at] for at in here], in_sems)
    gr_ref[...] = gain_ref[...] * read_ref[...]
    head = lax.axis_index("head")
    square = jnp.zeros((tokens, 1), F32)
    weighted = jnp.zeros((tokens, 1), F32)
    writes = []
    for c in range(depth // cols):
        start = (head + c) % (depth // cols) * cols
        at = pl.ds(pl.multiple_of(start, cols), cols)
        total = dot(att_refs[0][...], w_refs[0][:, at])
        for att_ref, w_ref in zip(att_refs[1:], w_refs[1:]):
            total = total + dot(att_ref[...], w_ref[:, at])
        if c == 0:
            out_ref[...] = total
            writes = copies(
                [out_ref.at[row] for row in here], [update_hbm.at[row] for row in slots], out_sems
            )
            for read in reads:
                read.wait()
        hidden = x_ref[:, at].astype(F32) + total
        square = square + jnp.sum(hidden * hidden, axis=1, keepdims=True)
        weighted = weighted + jnp.sum(hidden * gr_ref[:, at], axis=1, keepdims=True)
    score = weighted * lax.rsqrt(square / depth + 1e-06)
    token = lax.broadcasted_iota(jnp.int32, (width, 1), 0).astype(F32)
    lane = lax.broadcasted_iota(jnp.int32, (1, LANES), 1)
    pooled = before[1][...] if before else jnp.zeros((1, LANES), F32)
    for slot, row in zip(found, here):
        second = (seg_ref[pl.ds(slot, 1), :] & 1).astype(F32)
        count_two = jnp.sum(second, axis=1, keepdims=True)
        count_one = width - count_two
        is_first = token < count_one
        part = score[row, :]
        mean_one = jnp.sum(jnp.where(is_first, part, 0.0), axis=0, keepdims=True) / count_one
        mean_two = jnp.sum(jnp.where(is_first, 0.0, part), axis=0, keepdims=True) / count_two
        pooled = jnp.where(lane == 2 * slot, mean_one, pooled)
        pooled = jnp.where(lane == 2 * slot + 1, mean_two, pooled)
    pooled_ref[...] = pooled[:, : pooled_ref.shape[1]]
    for write in writes:
        write.wait()


def call(kernel, out, ins, scratch=(), flops=0, bytes_accessed=0, **kwargs):
    return pl.pallas_call(
        kernel,
        out_shape=out,
        in_specs=ins,
        scratch_shapes=list(scratch),
        compiler_params=pltpu.CompilerParams(vmem_limit_bytes=LIMIT),
        cost_estimate=pl.CostEstimate(
            flops=flops, bytes_accessed=bytes_accessed, transcendentals=0
        ),
        **kwargs,
    )


def in_hbm(*arrays):
    return [pltpu.with_memory_space_constraint(array, pltpu.HBM) for array in arrays]


def partner(value, axis, k):
    count = lax.axis_size(axis)
    return lax.ppermute(value, axis, [(i, i ^ k) for i in range(count)])


def spread_merge(backs, own, pick, slots, bpq):
    cols = backs[0].shape[0] - EXTRA
    width = backs[0].shape[1] // 2
    heads = cols // DH
    parts = jnp.stack(backs).reshape(len(backs), cols + EXTRA, 2, width)
    parts = parts.transpose(0, 2, 1, 3).reshape(2 * len(backs), cols + EXTRA, width)
    order = jnp.argsort(pick, stable=True)
    parts = jnp.take(parts, order, axis=0).reshape(slots, bpq, cols + EXTRA, width)
    stats = parts[:, :, cols : cols + 3 * heads].astype(F32)
    stats = stats.reshape(slots, bpq, 3, heads, width).sum(axis=2)
    stats = jnp.concatenate([stats, own[:, None, cols : cols + heads]], axis=1)
    weight = jnp.exp(stats - jnp.max(stats, axis=1, keepdims=True))
    weight = weight / jnp.sum(weight, axis=1, keepdims=True)
    values = jnp.concatenate([parts[:, :, :cols].astype(F32), own[:, None, :cols]], axis=1)
    values = values.reshape(slots, bpq + 1, heads, DH, width)
    mixed = jnp.sum(values * weight[:, :, :, None, :], axis=1).reshape(slots, cols, width)
    mixed = mixed.transpose(0, 2, 1).astype(BF)
    return [mixed[2 * k : 2 * k + 2].reshape(2 * width, cols) for k in range(slots // 2)]


def body(
    doc_x, doc_seg, doc_query, doc_var, query_len, block_perm, cache_k, cache_v, cache_var,
    w_query, w_key, w_value, w_out, var_bias, norm_gain, readout,
):
    rows, depth = doc_x.shape
    cols = w_query.shape[1]
    blocks = lax.axis_size("blk")
    head_count = lax.axis_size("head")
    bpq = blocks // QUERIES
    slots = QUERIES
    width = rows // slots
    chunks = blocks // 2
    cache_rows = cache_k.shape[0]
    seg = doc_seg.reshape(slots, width)
    var = doc_var.reshape(slots, width)
    table = np.concatenate(offset_tables(width), axis=0)
    cache_var = cache_var.reshape(cache_rows // LANES, LANES)
    sds = jax.ShapeDtypeStruct
    i32 = jnp.int32
    chunk_shape = sds((2 * width + EXTRA, cols), BF)
    base = pltpu.VMEM((5, slots, width), F32)

    pick, *queries = call(
        functools.partial(query_kernel, bpq, chunks),
        [sds((blocks,), i32)] + [chunk_shape] * chunks,
        [HBM] * 8,
        [pltpu.SMEM(ref.shape, i32) for ref in (doc_query, query_len, block_perm)]
        + [
            pltpu.VMEM(seg.shape, i32), pltpu.VMEM(var.shape, i32),
            pltpu.VMEM(table.shape, F32), pltpu.VMEM(doc_x.shape, BF),
            pltpu.VMEM(w_query.shape, BF), base, pltpu.VMEM((rows, cols), F32), DMA((8,)),
        ],
        flops=2 * rows * depth * cols,
        bytes_accessed=2 * rows * depth,
        out_specs=[SMEM] + [VMEM] * chunks,
        name="query",
    )(*in_hbm(doc_query, query_len, block_perm, seg, var, jnp.asarray(table), doc_x, w_query))

    asked = [queries[0]] + [partner(queries[k], "blk", 2 * k) for k in range(1, chunks)]

    packed, w_own = call(
        pack_kernel,
        [sds((2 * cache_rows + EXTRA, cols), BF), sds(w_out.shape, BF)],
        [HBM] * 4 + [ANY],
        [pltpu.VMEM(cache_v.shape, BF), pltpu.VMEM(cache_var.shape, i32), DMA((4,))],
        bytes_accessed=8 * cache_rows * cols,
        out_specs=[VMEM, VMEM],
        name="pack",
    )(*in_hbm(cache_k, cache_v, cache_var, w_out), pick)
    packed_other = partner(packed, "blk", 1)
    w_parts = [w_own] + [partner(w_own, "head", r) for r in range(1, head_count)]

    if bpq == 1:
        home = pick
        home_queries = queries
    else:
        home = jnp.arange(slots, dtype=i32)
        every = jnp.stack([q[: 2 * width] for q in queries]).reshape(blocks, width, cols)
        every = jnp.take(every, jnp.argsort(pick, stable=True)[::bpq], axis=0)
        home_queries = [
            every[2 * k : 2 * k + 2].reshape(2 * width, cols) for k in range(slots // 2)
        ]

    own = call(
        own_kernel,
        sds((slots, cols + 8, width), F32),
        [SMEM] * 4 + [VMEM] * 6 + [ANY] + [VMEM] * len(home_queries),
        [base, pltpu.VMEM((rows, cols), F32), pltpu.VMEM((rows, cols), F32)],
        flops=6 * rows * depth * cols,
        bytes_accessed=8 * rows * depth,
        out_specs=VMEM,
        name="own_documents",
    )(
        doc_query, query_len, var_bias, home, doc_x, w_key, w_value, seg, var, table, packed,
        *home_queries,
    )

    def from_cache(query):
        return call(
            functools.partial(cache_kernel, bpq),
            chunk_shape,
            [SMEM] * 3 + [VMEM] * 3 + [ANY],
            flops=16 * width * cache_rows * cols,
            bytes_accessed=8 * cache_rows * cols,
            out_specs=VMEM,
            name="cache_part",
        )(query_len, block_perm, var_bias, query, packed, packed_other, own)

    parts = [from_cache(query) for query in asked]
    backs = [parts[0]] + [partner(parts[k], "blk", 2 * k) for k in range(1, chunks)]

    groups = [[k] for k in range(slots // 2)]
    if bpq == 1:
        attended = [
            call(
                functools.partial(merge_kernel, [2 * k for k in group]),
                sds((2 * width * len(group), cols), BF),
                [VMEM] * (len(group) + 1),
                bytes_accessed=4 * rows * cols,
                out_specs=VMEM,
                name="merge",
            )(*[backs[k] for k in group], own)
            for group in groups
        ]
    else:
        attended = spread_merge(backs, own, pick, slots, bpq)
        attended = [jnp.concatenate([attended[k] for k in group]) for group in groups]

    gain, read = norm_gain.reshape(1, depth), readout.reshape(1, depth)
    chained = []
    for group, own_part in zip(groups, attended):
        atts = [own_part] + [partner(own_part, "head", r) for r in range(1, head_count)]
        places = 2 * len(group)
        last = group is groups[-1]
        chained = call(
            functools.partial(output_kernel, head_count, [2 * k for k in group], last),
            [sds((rows, cols), F32), sds((1, 2 * slots if last else LANES), F32)],
            [SMEM] + [VMEM] * (2 * head_count) + [HBM] + [VMEM] * 3 + [HBM, VMEM][: len(chained)],
            [
                pltpu.VMEM((places * width, depth), BF), pltpu.VMEM((1, depth), F32),
                pltpu.VMEM((places * width, cols), F32), DMA((places,)), DMA((places,)),
            ],
            flops=4 * places * width * depth * depth,
            bytes_accessed=2 * depth * depth,
            out_specs=[HBM, VMEM],
            input_output_aliases={5 + 2 * head_count: 0} if chained else {},
            name="output",
        )(home, *atts, *w_parts, *in_hbm(doc_x), seg, gain, read, *chained)
    update, pooled = chained
    return (update, pooled.reshape(2 * slots))


def solution(mesh):
    return jax.shard_map(
        body,
        mesh=mesh,
        in_specs=(
            P("blk", None), P("blk"), P(), P("blk"), P(), P(), P("blk", "head"),
            P("blk", "head"), P("blk"), P(None, "head"), P(None, "head"), P(None, "head"),
            P("head", None), P(None, "head"), P(), P(),
        ),
        out_specs=(P("blk", "head"), P("blk")),
        check_vma=False,
    )
```

```python
import functools

import jax
import jax.numpy as jnp
import numpy as np
from jax import lax
from jax.experimental import pallas as pl
from jax.experimental.pallas import tpu as pltpu
from jax.sharding import PartitionSpec as P

DH = 64
QUERIES = 8
LANES = 128
EXTRA = 16
NEVER = -1e30
BF = jnp.bfloat16
F32 = jnp.float32
VMEM = pl.BlockSpec(memory_space=pltpu.VMEM)
SMEM = pl.BlockSpec(memory_space=pltpu.SMEM)
HBM = pl.BlockSpec(memory_space=pltpu.HBM)
ANY = pl.BlockSpec(memory_space=pl.ANY)
DMA = pltpu.SemaphoreType.DMA
GROUPS = [[0, 1], [2], [3]]
LIMIT = 32 * 1024 * 1024


def offset_tables(slot_rows):
    half = DH // 2
    freq = (10000.0 ** (-np.arange(half, dtype=np.float64) / half)).astype(np.float32)
    lane_freq = np.tile(freq, LANES // half)
    angles = np.arange(slot_rows, dtype=np.float64)[:, None] * lane_freq[None, :].astype(np.float64)
    sign = np.where(np.arange(LANES) % DH < half, -1.0, 1.0).astype(np.float32)
    rows = np.zeros((8, LANES), np.float32)
    rows[0] = lane_freq
    rows[1] = sign
    return np.cos(angles).astype(np.float32), np.sin(angles).astype(np.float32), rows


def dot(a, b):
    return jnp.dot(a, b, preferred_element_type=F32)


def dot_t(a, b):
    return lax.dot_general(a, b, (((1,), (1,)), ((), ())), preferred_element_type=F32)


def slot_of(p, doc_query, block_perm, slots, bpq):
    blk = lax.axis_index("blk")
    wanted = block_perm[blk ^ p] // bpq
    slot = jnp.int32(0)
    for j in range(slots):
        slot = slot + jnp.where(doc_query[blk * 2 * slots + 2 * j] == wanted, j, 0)
    return slot


def start_tables(doc_query, query_len, seg_ref, rows_ref, base_ref):
    slots, width = seg_ref.shape
    blk = lax.axis_index("blk")
    row = lax.broadcasted_iota(jnp.int32, (slots, width), 0)
    length = jnp.zeros((slots, width), F32)
    for j in range(slots):
        value = query_len[doc_query[blk * 2 * slots + 2 * j]].astype(F32)
        length = jnp.where(row == j, value, length)
    second = (seg_ref[...] & 1).astype(F32)
    count = width - jnp.sum(second, axis=1, keepdims=True)
    count = jnp.broadcast_to(count, (slots, width))
    freq = rows_ref[0:1, :]
    one, two = length * freq, (length - count) * freq
    base_ref[0] = jnp.cos(one)
    base_ref[1] = jnp.sin(one)
    base_ref[2] = jnp.cos(two)
    base_ref[3] = jnp.sin(two)
    base_ref[4] = count


def slot_tables(slot, base_ref, cos_ref, sin_ref, rows_ref):
    shape = cos_ref.shape
    rows = [base_ref[i, pl.ds(slot, 1), :] for i in range(5)]
    token = lax.broadcasted_iota(jnp.int32, shape, 0).astype(F32)
    first = token < rows[4]
    base_cos = jnp.where(first, rows[0], rows[2])
    base_sin = jnp.where(first, rows[1], rows[3])
    off_cos, off_sin = cos_ref[...], sin_ref[...]
    cos = base_cos * off_cos - base_sin * off_sin
    sin = (base_sin * off_cos + base_cos * off_sin) * rows_ref[1:2, :]
    return cos, sin


def turn(value, cos, sin):
    lane = lax.broadcasted_iota(jnp.int32, cos.shape, 1)
    low = lane % DH < DH // 2
    parts = []
    for at in range(0, value.shape[1], LANES):
        part = value[:, at : at + LANES]
        other = jnp.where(
            low, pltpu.roll(part, LANES - DH // 2, 1), pltpu.roll(part, DH // 2, 1)
        )
        parts.append(part * cos + other * sin)
    return jnp.concatenate(parts, axis=1)


def copies(sources, targets, sems):
    moves = [
        pltpu.make_async_copy(source, target, sems.at[i])
        for i, (source, target) in enumerate(zip(sources, targets))
    ]
    for move in moves:
        move.start()
    return moves


def query_kernel(bpq, chunks, *refs):
    sources, refs = refs[:11], refs[11:]
    pick_ref, base_ref, usable_ref, packed_ref = refs[:4]
    q_refs, refs = refs[4 : 4 + chunks], refs[4 + chunks :]
    targets, (y_ref, sems) = list(refs[:10]), refs[10:]
    rows, cols = sources[10].shape
    moves = copies(sources, targets + [packed_ref.at[0:rows]], sems)
    doc_query, query_len, block_perm, seg_ref, var_ref, table_ref, key_var_ref = targets[:7]
    x_ref, w_ref, v_ref = targets[7:]
    slots, width = seg_ref.shape
    cos_ref, sin_ref = table_ref.at[0:width], table_ref.at[width : 2 * width]
    rows_ref = table_ref.at[2 * width :]
    for move in moves[:7]:
        move.wait()
    start_tables(doc_query, query_len, seg_ref, rows_ref, base_ref)
    row = lax.broadcasted_iota(jnp.int32, usable_ref.shape, 0)
    usable = jnp.zeros(usable_ref.shape, jnp.int32)
    for j in range(2):
        block = block_perm[lax.axis_index("blk") ^ j]
        here = query_len[block // bpq] - block % bpq * rows
        usable = jnp.where(row == j, here, usable)
    usable_ref[...] = usable
    parts = rows // LANES
    key_var = key_var_ref[...].astype(F32)
    key_var = jnp.concatenate([key_var, jnp.zeros((EXTRA - parts, LANES), F32)], axis=0)
    packed_ref[2 * rows :, :] = jnp.concatenate([key_var, key_var], axis=1).astype(BF)
    for move in moves[7:9]:
        move.wait()
    y_ref[...] = dot(x_ref[...], w_ref[...])
    moves[9].wait()
    for i in range(rows // cols):
        block = v_ref[i * cols : (i + 1) * cols, :].astype(F32)
        packed_ref[rows + i * cols : rows + (i + 1) * cols, :] = block.T.astype(BF)
    for k, q_ref in enumerate(q_refs):
        for j in range(2):
            slot = slot_of(2 * k + j, doc_query, block_perm, slots, bpq)
            pick_ref[2 * k + j] = slot
            cos, sin = slot_tables(slot, base_ref, cos_ref, sin_ref, rows_ref)
            at = pl.ds(pl.multiple_of(slot * width, width), width)
            turned = turn(y_ref[at, :], cos, sin)
            q_ref[j * width : (j + 1) * width, :] = (turned * 0.125).astype(BF)
            var = var_ref[pl.ds(slot, 1), :].astype(F32)
            q_ref[2 * width :, j * width : (j + 1) * width] = jnp.broadcast_to(
                var, (EXTRA, width)
            ).astype(BF)
    moves[10].wait()


def by_head(query):
    lane = lax.broadcasted_iota(jnp.int32, query.shape, 1) // DH
    heads = query.shape[1] // DH
    return jnp.concatenate(
        [jnp.where(lane == h, query, jnp.zeros_like(query)) for h in range(heads)], axis=0
    )


def fold(value, op):
    while value.shape[0] > 8:
        half = value.shape[0] // 2
        value = op(value[:half], value[half:])
    return value


def attend(scores, same, allowed, bias_ref, values, out_ref, at):
    width = same.shape[1]
    stats = []
    for h in range(scores.shape[1] // width):
        part = scores[:, h * width : (h + 1) * width]
        part = part + jnp.where(same, bias_ref[0:1, h : h + 1], bias_ref[1:2, h : h + 1])
        part = jnp.where(allowed, part, NEVER)
        peak = jnp.max(fold(part, jnp.maximum), axis=0, keepdims=True)
        weight = jnp.exp(part - peak)
        total = jnp.sum(fold(weight, jnp.add), axis=0, keepdims=True)
        weight = weight.astype(BF)
        mixed = None
        key = 0
        for value in values:
            keys = value.shape[1]
            term = dot(value[h * DH : (h + 1) * DH, :], weight[key : key + keys, :])
            mixed = term if mixed is None else mixed + term
            key += keys
        mixed = mixed * (1.0 / total)
        out_ref[h * DH : (h + 1) * DH, at] = mixed.astype(out_ref.dtype)
        stats.append(peak + jnp.log(total))
    return stats


def cache_kernel(usable_ref, bias_ref, q_ref, own_ref, other_ref, *refs):
    out_ref = refs[-1]
    width = q_ref.shape[0] // 2 - EXTRA // 2
    cols = q_ref.shape[1]
    rows = (own_ref.shape[0] - EXTRA) // 2
    for j, ref in enumerate((own_ref, other_ref)):
        var = ref[2 * rows :, 0:LANES].astype(F32)
        var = jnp.concatenate([var, jnp.zeros((LANES - EXTRA, LANES), F32)], axis=0).T
        key_var = jnp.concatenate(
            [jnp.broadcast_to(var[:, i : i + 1], (LANES, width)) for i in range(rows // LANES)],
            axis=0,
        )
        tok_var = q_ref[2 * width :, j * width : (j + 1) * width].astype(F32)[0:1, :]
        same = key_var == tok_var
        allowed = lax.broadcasted_iota(jnp.int32, (rows, width), 0) < usable_ref[j : j + 1, :]
        scores = dot_t(ref[0:rows, :], by_head(q_ref[j * width : (j + 1) * width, :]))
        values = [ref[rows + i * cols : rows + (i + 1) * cols, :] for i in range(rows // cols)]
        at = slice(j * width, (j + 1) * width)
        stats = attend(scores, same, allowed, bias_ref, values, out_ref, at)
        full = jnp.concatenate(stats, axis=0)
        high = full.astype(BF).astype(F32)
        middle = (full - high).astype(BF).astype(F32)
        low = full - high - middle
        pad = jnp.zeros((EXTRA - 3 * len(stats), width), F32)
        out_ref[cols:, at] = jnp.concatenate([high, middle, low, pad], axis=0).astype(BF)


def own_kernel(
    home_any, bias_ref, x_ref, wk_ref, wv_ref, var_ref, table_ref, base_ref, after,
    *refs
):
    del after
    out_ref, x_home_ref, k_ref, v_ref, home_ref, sem = refs[-6:]
    q_refs = refs[:-6]
    slots, width = var_ref.shape
    cols = wk_ref.shape[1]
    home_move = pltpu.make_async_copy(home_any, home_ref, sem)
    home_move.start()
    cos_ref, sin_ref = table_ref.at[0:width], table_ref.at[width : 2 * width]
    rows_ref = table_ref.at[2 * width :]
    k_ref[...] = dot(x_ref[...], wk_ref[...])
    v_ref[...] = dot(x_ref[...], wv_ref[...])
    home_move.wait()
    for n in range(slots):
        slot = home_ref[n]
        cos, sin = slot_tables(slot, base_ref, cos_ref, sin_ref, rows_ref)
        at = pl.ds(pl.multiple_of(slot * width, width), width)
        x_home_ref[n * width : (n + 1) * width, :] = x_ref[at, :]
        key = turn(k_ref[at, :], cos, sin).astype(BF)
        value = v_ref[at, :].T.astype(BF)
        query = q_refs[n // 2][n % 2 * width : (n % 2 + 1) * width, :]
        scores = dot_t(key, by_head(query))
        var = jnp.broadcast_to(var_ref[pl.ds(slot, 1), :].astype(F32), (width, width))
        same = var.T == var
        count = base_ref[4, pl.ds(slot, 1), :]
        key_second = lax.broadcasted_iota(jnp.int32, (width, width), 0).astype(F32) >= count
        tok_second = lax.broadcasted_iota(jnp.int32, (width, width), 1).astype(F32) >= count
        allowed = jnp.logical_not(jnp.logical_xor(key_second, tok_second))
        part_ref = out_ref.at[n]
        stats = attend(scores, same, allowed, bias_ref, [value], part_ref, slice(None))
        stats = jnp.concatenate(stats + [jnp.zeros((8 - len(stats), width), F32)], axis=0)
        part_ref[cols:, :] = stats


def merge_kernel(firsts, *refs):
    own_ref, after, out_ref = refs[-3:]
    del after
    for i, (first, got_ref) in enumerate(zip(firsts, refs)):
        cols = got_ref.shape[0] - EXTRA
        heads = cols // DH
        width = got_ref.shape[1] // 2
        for j in range(2):
            at = slice(j * width, (j + 1) * width)
            stats = got_ref[cols:, at].astype(F32)
            there = stats[0:heads] + stats[heads : 2 * heads] + stats[2 * heads : 3 * heads]
            here = own_ref[first + j, cols : cols + heads, :]
            peak = jnp.maximum(there, here)
            there, here = jnp.exp(there - peak), jnp.exp(here - peak)
            inverse = 1.0 / (there + here)
            there, here = there * inverse, here * inverse
            parts = []
            for h in range(heads):
                row = slice(h * DH, (h + 1) * DH)
                parts.append(
                    got_ref[row, at].astype(F32) * there[h : h + 1]
                    + own_ref[first + j, row, :] * here[h : h + 1]
                )
            to = slice((2 * i + j) * width, (2 * i + j + 1) * width)
            out_ref[to, :] = jnp.concatenate(parts, axis=0).T.astype(BF)


def output_kernel(firsts, home_any, *refs):
    att_refs, w_refs = refs[:4], refs[4:8]
    x_ref, base_ref, gain_ref, read_ref = refs[8:12]
    before = refs[12:-6]
    update_hbm, pooled_ref, gr_ref, out_ref, home_ref, sems = refs[-6:]
    tokens, cols = att_refs[0].shape
    depth = w_refs[0].shape[1]
    width = tokens // (2 * len(firsts))
    places = [first + j for first in firsts for j in range(2)]
    here = [slice(i * width, (i + 1) * width) for i in range(len(places))]
    home_move = pltpu.make_async_copy(home_any, home_ref, sems.at[len(places)])
    home_move.start()
    gr_ref[...] = gain_ref[...] * read_ref[...]
    head = lax.axis_index("head")
    square = jnp.zeros((tokens, LANES), F32)
    weighted = jnp.zeros((tokens, LANES), F32)
    for c in range(depth // cols):
        start = (head + c) % (depth // cols) * cols
        at = pl.ds(pl.multiple_of(start, cols), cols)
        total = dot(att_refs[0][...], w_refs[0][:, at])
        for att_ref, w_ref in zip(att_refs[1:], w_refs[1:]):
            total = total + dot(att_ref[...], w_ref[:, at])
        if c == 0:
            out_ref[...] = total
            home_move.wait()
            found = [home_ref[place] for place in places]
            slots = [pl.ds(pl.multiple_of(slot * width, width), width) for slot in found]
            writes = copies(
                [out_ref.at[row] for row in here], [update_hbm.at[row] for row in slots], sems
            )
        hidden = x_ref[places[0] * width : (places[-1] + 1) * width, at].astype(F32) + total
        scaled = hidden * gr_ref[:, at]
        hidden = hidden * hidden
        for lane in range(0, cols, LANES):
            square = square + hidden[:, lane : lane + LANES]
            weighted = weighted + scaled[:, lane : lane + LANES]
    square = jnp.sum(square, axis=1, keepdims=True)
    weighted = jnp.sum(weighted, axis=1, keepdims=True)
    score = weighted * lax.rsqrt(square / depth + 1e-06)
    token = lax.broadcasted_iota(jnp.int32, (width, 1), 0).astype(F32)
    lane = lax.broadcasted_iota(jnp.int32, (1, LANES), 1)
    pooled = before[1][...] if before else jnp.zeros((1, LANES), F32)
    for slot, row in zip(found, here):
        count_one = base_ref[4, pl.ds(slot, 1), 0:1]
        is_first = token < count_one
        part = score[row, :]
        sum_one = jnp.sum(jnp.where(is_first, part, 0.0), axis=0, keepdims=True)
        sum_two = jnp.sum(jnp.where(is_first, 0.0, part), axis=0, keepdims=True)
        pooled = jnp.where(lane == 2 * slot, sum_one / count_one, pooled)
        pooled = jnp.where(lane == 2 * slot + 1, sum_two / (width - count_one), pooled)
    pooled_ref[...] = pooled[:, : pooled_ref.shape[1]]
    for write in writes:
        write.wait()


def call(kernel, out, ins, scratch=(), work=1, **kwargs):
    return pl.pallas_call(
        kernel,
        out_shape=out,
        in_specs=ins,
        scratch_shapes=list(scratch),
        compiler_params=pltpu.CompilerParams(vmem_limit_bytes=LIMIT),
        cost_estimate=pl.CostEstimate(
            flops=int(work * 1e9), bytes_accessed=0, transcendentals=0
        ),
        **kwargs,
    )


def in_hbm(*arrays):
    return [pltpu.with_memory_space_constraint(jnp.asarray(a), pltpu.HBM) for a in arrays]


def partner(value, axis, k):
    count = lax.axis_size(axis)
    return lax.ppermute(value, axis, [(i, i ^ k) for i in range(count)])


def hop(value, even, odd):
    heads, blocks = lax.axis_size("head"), lax.axis_size("blk")
    pairs = []
    for h in range(heads):
        for b in range(blocks):
            pairs.append((h * blocks + b, (h ^ (odd if b % 2 else even)) * blocks + b))
    return lax.ppermute(value, ("head", "blk"), pairs)


def spread_merge(backs, own, pick, slots, bpq):
    cols = backs[0].shape[0] - EXTRA
    width = backs[0].shape[1] // 2
    heads = cols // DH
    parts = jnp.stack(backs).reshape(len(backs), cols + EXTRA, 2, width)
    parts = parts.transpose(0, 2, 1, 3).reshape(2 * len(backs), cols + EXTRA, width)
    order = jnp.argsort(pick, stable=True)
    parts = jnp.take(parts, order, axis=0).reshape(slots, bpq, cols + EXTRA, width)
    stats = parts[:, :, cols : cols + 3 * heads].astype(F32)
    stats = stats.reshape(slots, bpq, 3, heads, width).sum(axis=2)
    stats = jnp.concatenate([stats, own[:, None, cols : cols + heads]], axis=1)
    weight = jnp.exp(stats - jnp.max(stats, axis=1, keepdims=True))
    weight = weight / jnp.sum(weight, axis=1, keepdims=True)
    values = jnp.concatenate([parts[:, :, :cols].astype(F32), own[:, None, :cols]], axis=1)
    values = values.reshape(slots, bpq + 1, heads, DH, width)
    mixed = jnp.sum(values * weight[:, :, :, None, :], axis=1).reshape(slots, cols, width)
    mixed = mixed.transpose(0, 2, 1).astype(BF)
    return [mixed[2 * k : 2 * k + 2].reshape(2 * width, cols) for k in range(slots // 2)]


def body(
    doc_x, doc_seg, doc_query, doc_var, query_len, block_perm, cache_k, cache_v, cache_var,
    w_query, w_key, w_value, w_out, var_bias, norm_gain, readout,
):
    rows, depth = doc_x.shape
    cols = w_query.shape[1]
    blocks = lax.axis_size("blk")
    bpq = blocks // QUERIES
    slots = QUERIES
    width = rows // slots
    chunks = blocks // 2
    cache_rows = cache_k.shape[0]
    seg = doc_seg.reshape(slots, width)
    var = doc_var.reshape(slots, width)
    table = np.concatenate(offset_tables(width), axis=0)
    cache_var = cache_var.reshape(cache_rows // LANES, LANES)
    sds = jax.ShapeDtypeStruct
    i32 = jnp.int32
    chunk_shape = sds((2 * width + EXTRA, cols), BF)
    base_shape = sds((5, slots, width), F32)

    w_first = hop(w_out, 1, 2)
    w_second = partner(w_first, "blk", 1)
    w_third = hop(w_first, 2, 1)

    pick, base, usable, packed, *queries = call(
        functools.partial(query_kernel, bpq, chunks),
        [
            sds((blocks,), i32), base_shape, sds((8, width), i32),
            sds((2 * cache_rows + EXTRA, cols), BF),
        ]
        + [chunk_shape] * chunks,
        [HBM] * 11,
        [pltpu.SMEM(ref.shape, i32) for ref in (doc_query, query_len, block_perm)]
        + [pltpu.VMEM(ref.shape, i32) for ref in (seg, var)]
        + [pltpu.VMEM(table.shape, F32), pltpu.VMEM(cache_var.shape, i32)]
        + [pltpu.VMEM(ref.shape, BF) for ref in (doc_x, w_query, cache_v)]
        + [pltpu.VMEM((rows, cols), F32), DMA((11,))],
        out_specs=[SMEM] + [VMEM] * (chunks + 3),
        work=3.5,
        name="query",
    )(
        *in_hbm(
            doc_query, query_len, block_perm, seg, var, table, cache_var, doc_x, w_query,
            cache_v, cache_k,
        )
    )

    asked = [queries[0]] + [partner(queries[k], "blk", 2 * k) for k in range(1, chunks)]
    packed_other = partner(packed, "blk", 1)

    if bpq == 1:
        home = pick
        home_queries = queries
    else:
        home = jnp.arange(slots, dtype=i32)
        every = jnp.stack([q[: 2 * width] for q in queries]).reshape(blocks, width, cols)
        every = jnp.take(every, jnp.argsort(pick, stable=True)[::bpq], axis=0)
        home_queries = [
            every[2 * k : 2 * k + 2].reshape(2 * width, cols) for k in range(slots // 2)
        ]

    own, x_home = call(
        own_kernel,
        [sds((slots, cols + 8, width), F32), sds((rows, depth), BF)],
        [ANY] + [VMEM] * 7 + [ANY] + [VMEM] * len(home_queries),
        [
            pltpu.VMEM((rows, cols), F32), pltpu.VMEM((rows, cols), F32),
            pltpu.SMEM(home.shape, i32), DMA,
        ],
        out_specs=[VMEM] * 2,
        work=4.0,
        name="own_documents",
    )(home, var_bias, doc_x, w_key, w_value, var, table, base, packed_other, *home_queries)

    parts = []
    for k, query in enumerate(asked):
        after = [parts[-1] if parts else own]
        if k == chunks - 1:
            after += [w_second, w_third]
        part = call(
            cache_kernel,
            chunk_shape,
            [VMEM] * 5 + [ANY] * len(after),
            out_specs=VMEM,
            work=1.5,
            name="cache_part",
        )(usable, var_bias, query, packed, packed_other, *after)
        parts.append(part)
    backs = [parts[0]] + [partner(parts[k], "blk", 2 * k) for k in range(1, chunks)]

    groups = GROUPS
    if bpq == 1:
        attended = [
            call(
                functools.partial(merge_kernel, [2 * k for k in group]),
                sds((2 * width * len(group), cols), BF),
                [VMEM] * (len(group) + 1) + [ANY],
                out_specs=VMEM,
                work=0.2,
            name="merge",
            )(*[backs[k] for k in group], own, parts[-1])
            for group in groups
        ]
    else:
        attended = spread_merge(backs, own, pick, slots, bpq)
        attended = [jnp.concatenate([attended[k] for k in group]) for group in groups]

    gain, read = norm_gain.reshape(1, depth), readout.reshape(1, depth)
    chained = []
    for group, own_part in zip(groups, attended):
        near = hop(own_part, 1, 2)
        atts = [own_part, near, hop(own_part, 2, 1), hop(near, 2, 1)]
        places = 2 * len(group)
        last = group is groups[-1]
        chained = call(
            functools.partial(output_kernel, [2 * k for k in group]),
            [sds((rows, cols), F32), sds((1, 2 * slots if last else LANES), F32)],
            [ANY] + [VMEM] * 12 + [HBM, VMEM][: len(chained)],
            [
                pltpu.VMEM((1, depth), F32), pltpu.VMEM((places * width, cols), F32),
                pltpu.SMEM(home.shape, i32), DMA((places + 1,)),
            ],
            out_specs=[HBM, VMEM],
            input_output_aliases={13: 0} if chained else {},
            work=2.5,
            name="output",
        )(home, *atts, w_out, w_first, w_second, w_third, x_home, base, gain, read, *chained)
    update, pooled = chained
    return (update, pooled.reshape(2 * slots))


def solution(mesh):
    return jax.shard_map(
        body,
        mesh=mesh,
        in_specs=(
            P("blk", None), P("blk"), P(), P("blk"), P(), P(), P("blk", "head"),
            P("blk", "head"), P("blk"), P(None, "head"), P(None, "head"), P(None, "head"),
            P("head", None), P(None, "head"), P(), P(),
        ),
        out_specs=(P("blk", "head"), P("blk")),
        check_vma=False,
    )
```

```python
import functools

import jax
import jax.numpy as jnp
import numpy as np
from jax import lax
from jax.experimental import pallas as pl
from jax.experimental.pallas import tpu as pltpu
from jax.sharding import PartitionSpec as P

DH = 64
QUERIES = 8
LANES = 128
EXTRA = 16
NEVER = -1e30
BF = jnp.bfloat16
F32 = jnp.float32
VMEM = pl.BlockSpec(memory_space=pltpu.VMEM)
SMEM = pl.BlockSpec(memory_space=pltpu.SMEM)
HBM = pl.BlockSpec(memory_space=pltpu.HBM)
ANY = pl.BlockSpec(memory_space=pl.ANY)
DMA = pltpu.SemaphoreType.DMA
GROUPS = [[0, 1], [2, 3]]
LIMIT = 32 * 1024 * 1024


def offset_tables(slot_rows):
    half = DH // 2
    freq = (10000.0 ** (-np.arange(half, dtype=np.float64) / half)).astype(np.float32)
    lane_freq = np.tile(freq, LANES // half)
    angles = np.arange(slot_rows, dtype=np.float64)[:, None] * lane_freq[None, :].astype(np.float64)
    sign = np.where(np.arange(LANES) % DH < half, -1.0, 1.0).astype(np.float32)
    rows = np.zeros((8, LANES), np.float32)
    rows[0] = lane_freq
    rows[1] = sign
    return np.cos(angles).astype(np.float32), np.sin(angles).astype(np.float32), rows


def dot(a, b):
    return jnp.dot(a, b, preferred_element_type=F32)


def dot_t(a, b):
    return lax.dot_general(a, b, (((1,), (1,)), ((), ())), preferred_element_type=F32)


def slot_of(p, doc_query, block_perm, slots, bpq):
    blk = lax.axis_index("blk")
    wanted = block_perm[blk ^ p] // bpq
    slot = jnp.int32(0)
    for j in range(slots):
        slot = slot + jnp.where(doc_query[blk * 2 * slots + 2 * j] == wanted, j, 0)
    return slot


def start_tables(doc_query, query_len, seg_ref, rows_ref, base_ref):
    slots, width = seg_ref.shape
    blk = lax.axis_index("blk")
    row = lax.broadcasted_iota(jnp.int32, (slots, width), 0)
    length = jnp.zeros((slots, width), F32)
    for j in range(slots):
        value = query_len[doc_query[blk * 2 * slots + 2 * j]].astype(F32)
        length = jnp.where(row == j, value, length)
    second = (seg_ref[...] & 1).astype(F32)
    count = width - jnp.sum(second, axis=1, keepdims=True)
    count = jnp.broadcast_to(count, (slots, width))
    freq = rows_ref[0:1, :]
    one, two = length * freq, (length - count) * freq
    base_ref[0] = jnp.cos(one)
    base_ref[1] = jnp.sin(one)
    base_ref[2] = jnp.cos(two)
    base_ref[3] = jnp.sin(two)
    base_ref[4] = count


def slot_tables(slot, base_ref, cos_ref, sin_ref, rows_ref):
    shape = cos_ref.shape
    rows = [base_ref[i, pl.ds(slot, 1), :] for i in range(5)]
    token = lax.broadcasted_iota(jnp.int32, shape, 0).astype(F32)
    first = token < rows[4]
    base_cos = jnp.where(first, rows[0], rows[2])
    base_sin = jnp.where(first, rows[1], rows[3])
    off_cos, off_sin = cos_ref[...], sin_ref[...]
    cos = base_cos * off_cos - base_sin * off_sin
    sin = (base_sin * off_cos + base_cos * off_sin) * rows_ref[1:2, :]
    return cos, sin


def turn(value, cos, sin):
    lane = lax.broadcasted_iota(jnp.int32, cos.shape, 1)
    low = lane % DH < DH // 2
    parts = []
    for at in range(0, value.shape[1], LANES):
        part = value[:, at : at + LANES]
        other = jnp.where(
            low, pltpu.roll(part, LANES - DH // 2, 1), pltpu.roll(part, DH // 2, 1)
        )
        parts.append(part * cos + other * sin)
    return jnp.concatenate(parts, axis=1)


def copies(sources, targets, sems):
    moves = [
        pltpu.make_async_copy(source, target, sems.at[i])
        for i, (source, target) in enumerate(zip(sources, targets))
    ]
    for move in moves:
        move.start()
    return moves


def query_kernel(bpq, order, *refs):
    chunks = len(order)
    sources, refs = refs[:11], refs[11:]
    pick_ref, base_ref, usable_ref, packed_ref = refs[:4]
    q_refs, refs = refs[4 : 4 + chunks], refs[4 + chunks :]
    targets, (y_ref, sems) = list(refs[:10]), refs[10:]
    rows, cols = sources[10].shape
    moves = copies(sources, targets + [packed_ref.at[0:rows]], sems)
    doc_query, query_len, block_perm, seg_ref, var_ref, table_ref, key_var_ref = targets[:7]
    x_ref, w_ref, v_ref = targets[7:]
    slots, width = seg_ref.shape
    cos_ref, sin_ref = table_ref.at[0:width], table_ref.at[width : 2 * width]
    rows_ref = table_ref.at[2 * width :]
    for move in moves[:7]:
        move.wait()
    start_tables(doc_query, query_len, seg_ref, rows_ref, base_ref)
    row = lax.broadcasted_iota(jnp.int32, usable_ref.shape, 0)
    usable = jnp.zeros(usable_ref.shape, jnp.int32)
    for j in range(2):
        block = block_perm[lax.axis_index("blk") ^ j]
        here = query_len[block // bpq] - block % bpq * rows
        usable = jnp.where(row == j, here, usable)
    usable_ref[...] = usable
    parts = rows // LANES
    key_var = key_var_ref[...].astype(F32)
    key_var = jnp.concatenate([key_var, jnp.zeros((EXTRA - parts, LANES), F32)], axis=0)
    packed_ref[2 * rows :, :] = jnp.concatenate([key_var, key_var], axis=1).astype(BF)
    for move in moves[7:9]:
        move.wait()
    y_ref[...] = dot(x_ref[...], w_ref[...])
    moves[9].wait()
    for i in range(rows // cols):
        block = v_ref[i * cols : (i + 1) * cols, :].astype(F32)
        packed_ref[rows + i * cols : rows + (i + 1) * cols, :] = block.T.astype(BF)
    for k, q_ref in enumerate(q_refs):
        for j in range(2):
            slot = slot_of(2 * order[k] + j, doc_query, block_perm, slots, bpq)
            pick_ref[2 * k + j] = slot
            cos, sin = slot_tables(slot, base_ref, cos_ref, sin_ref, rows_ref)
            at = pl.ds(pl.multiple_of(slot * width, width), width)
            turned = turn(y_ref[at, :], cos, sin)
            q_ref[j * width : (j + 1) * width, :] = (turned * 0.125).astype(BF)
            var = var_ref[pl.ds(slot, 1), :].astype(F32)
            q_ref[2 * width :, j * width : (j + 1) * width] = jnp.broadcast_to(
                var, (EXTRA, width)
            ).astype(BF)
    moves[10].wait()


def by_head(query):
    lane = lax.broadcasted_iota(jnp.int32, query.shape, 1) // DH
    heads = query.shape[1] // DH
    return jnp.concatenate(
        [jnp.where(lane == h, query, jnp.zeros_like(query)) for h in range(heads)], axis=0
    )


def fold(value, op):
    while value.shape[0] > 8:
        half = value.shape[0] // 2
        value = op(value[:half], value[half:])
    return value


def attend(scores, same, allowed, bias_ref, values, out_ref, at):
    width = same.shape[1]
    stats = []
    for h in range(scores.shape[1] // width):
        part = scores[:, h * width : (h + 1) * width]
        part = part + jnp.where(same, bias_ref[0:1, h : h + 1], bias_ref[1:2, h : h + 1])
        part = jnp.where(allowed, part, NEVER)
        peak = jnp.max(fold(part, jnp.maximum), axis=0, keepdims=True)
        weight = jnp.exp(part - peak)
        total = jnp.sum(fold(weight, jnp.add), axis=0, keepdims=True)
        weight = weight.astype(BF)
        mixed = None
        key = 0
        for value in values:
            keys = value.shape[1]
            term = dot(value[h * DH : (h + 1) * DH, :], weight[key : key + keys, :])
            mixed = term if mixed is None else mixed + term
            key += keys
        mixed = mixed * (1.0 / total)
        out_ref[h * DH : (h + 1) * DH, at] = mixed.astype(out_ref.dtype)
        stats.append(peak + jnp.log(total))
    return stats


def cache_kernel(usable_ref, bias_ref, q_ref, own_ref, other_ref, *refs):
    out_ref = refs[-1]
    width = q_ref.shape[0] // 2 - EXTRA // 2
    cols = q_ref.shape[1]
    rows = (own_ref.shape[0] - EXTRA) // 2
    for j, ref in enumerate((own_ref, other_ref)):
        var = ref[2 * rows :, 0:LANES].astype(F32)
        var = jnp.concatenate([var, jnp.zeros((LANES - EXTRA, LANES), F32)], axis=0).T
        key_var = jnp.concatenate(
            [jnp.broadcast_to(var[:, i : i + 1], (LANES, width)) for i in range(rows // LANES)],
            axis=0,
        )
        tok_var = q_ref[2 * width :, j * width : (j + 1) * width].astype(F32)[0:1, :]
        same = key_var == tok_var
        allowed = lax.broadcasted_iota(jnp.int32, (rows, width), 0) < usable_ref[j : j + 1, :]
        scores = dot_t(ref[0:rows, :], by_head(q_ref[j * width : (j + 1) * width, :]))
        values = [ref[rows + i * cols : rows + (i + 1) * cols, :] for i in range(rows // cols)]
        at = slice(j * width, (j + 1) * width)
        stats = attend(scores, same, allowed, bias_ref, values, out_ref, at)
        full = jnp.concatenate(stats, axis=0)
        high = full.astype(BF).astype(F32)
        middle = (full - high).astype(BF).astype(F32)
        low = full - high - middle
        pad = jnp.zeros((EXTRA - 3 * len(stats), width), F32)
        out_ref[cols:, at] = jnp.concatenate([high, middle, low, pad], axis=0).astype(BF)


def own_kernel(
    home_any, bias_ref, x_ref, wk_ref, wv_ref, var_ref, table_ref, base_ref,
    *refs
):
    w_ref, out_ref, x_home_ref, w_copy_ref, k_ref, v_ref, home_ref, sem = refs[-8:]
    q_refs = refs[:-8]
    w_copy_ref[...] = w_ref[...]
    slots, width = var_ref.shape
    cols = wk_ref.shape[1]
    home_move = pltpu.make_async_copy(home_any, home_ref, sem)
    home_move.start()
    cos_ref, sin_ref = table_ref.at[0:width], table_ref.at[width : 2 * width]
    rows_ref = table_ref.at[2 * width :]
    k_ref[...] = dot(x_ref[...], wk_ref[...])
    v_ref[...] = dot(x_ref[...], wv_ref[...])
    home_move.wait()
    for n in range(slots):
        slot = home_ref[n]
        cos, sin = slot_tables(slot, base_ref, cos_ref, sin_ref, rows_ref)
        at = pl.ds(pl.multiple_of(slot * width, width), width)
        x_home_ref[n * width : (n + 1) * width, :] = x_ref[at, :]
        key = turn(k_ref[at, :], cos, sin).astype(BF)
        value = v_ref[at, :].T.astype(BF)
        query = q_refs[n // 2][n % 2 * width : (n % 2 + 1) * width, :]
        scores = dot_t(key, by_head(query))
        var = jnp.broadcast_to(var_ref[pl.ds(slot, 1), :].astype(F32), (width, width))
        same = var.T == var
        count = base_ref[4, pl.ds(slot, 1), :]
        key_second = lax.broadcasted_iota(jnp.int32, (width, width), 0).astype(F32) >= count
        tok_second = lax.broadcasted_iota(jnp.int32, (width, width), 1).astype(F32) >= count
        allowed = jnp.logical_not(jnp.logical_xor(key_second, tok_second))
        part_ref = out_ref.at[n]
        stats = attend(scores, same, allowed, bias_ref, [value], part_ref, slice(None))
        stats = jnp.concatenate(stats + [jnp.zeros((8 - len(stats), width), F32)], axis=0)
        part_ref[cols:, :] = stats


def merge_kernel(firsts, own_ref, *refs):
    out_ref = refs[-1]
    for i, (first, got_ref) in enumerate(zip(firsts, refs)):
        cols = got_ref.shape[0] - EXTRA
        heads = cols // DH
        width = got_ref.shape[1] // 2
        for j in range(2):
            at = slice(j * width, (j + 1) * width)
            stats = got_ref[cols:, at].astype(F32)
            there = stats[0:heads] + stats[heads : 2 * heads] + stats[2 * heads : 3 * heads]
            here = own_ref[first + j, cols : cols + heads, :]
            peak = jnp.maximum(there, here)
            there, here = jnp.exp(there - peak), jnp.exp(here - peak)
            inverse = 1.0 / (there + here)
            there, here = there * inverse, here * inverse
            parts = []
            for h in range(heads):
                row = slice(h * DH, (h + 1) * DH)
                parts.append(
                    got_ref[row, at].astype(F32) * there[h : h + 1]
                    + own_ref[first + j, row, :] * here[h : h + 1]
                )
            to = slice((2 * i + j) * width, (2 * i + j + 1) * width)
            out_ref[to, :] = jnp.concatenate(parts, axis=0).T.astype(BF)


def output_kernel(firsts, home_any, *refs):
    att_refs, w_refs = refs[:4], refs[4:8]
    x_ref, base_ref, gain_ref, read_ref = refs[8:12]
    before = refs[12:-6]
    update_hbm, pooled_ref, gr_ref, out_ref, home_ref, sems = refs[-6:]
    tokens, cols = att_refs[0].shape
    depth = w_refs[0].shape[1]
    width = tokens // (2 * len(firsts))
    places = [first + j for first in firsts for j in range(2)]
    here = [slice(i * width, (i + 1) * width) for i in range(len(places))]
    home_move = pltpu.make_async_copy(home_any, home_ref, sems.at[len(places)])
    home_move.start()
    gr_ref[...] = gain_ref[...] * read_ref[...]
    head = lax.axis_index("head")
    square = jnp.zeros((tokens, LANES), F32)
    weighted = jnp.zeros((tokens, LANES), F32)
    for c in range(depth // cols):
        start = (head + c) % (depth // cols) * cols
        at = pl.ds(pl.multiple_of(start, cols), cols)
        total = dot(att_refs[0][...], w_refs[0][:, at])
        for att_ref, w_ref in zip(att_refs[1:], w_refs[1:]):
            total = total + dot(att_ref[...], w_ref[:, at])
        if c == 0:
            out_ref[...] = total
            home_move.wait()
            found = [home_ref[place] for place in places]
            slots = [pl.ds(pl.multiple_of(slot * width, width), width) for slot in found]
            writes = copies(
                [out_ref.at[row] for row in here], [update_hbm.at[row] for row in slots], sems
            )
        hidden = x_ref[places[0] * width : (places[-1] + 1) * width, at].astype(F32) + total
        scaled = hidden * gr_ref[:, at]
        hidden = hidden * hidden
        for lane in range(0, cols, LANES):
            square = square + hidden[:, lane : lane + LANES]
            weighted = weighted + scaled[:, lane : lane + LANES]
    square = jnp.sum(square, axis=1, keepdims=True)
    weighted = jnp.sum(weighted, axis=1, keepdims=True)
    score = weighted * lax.rsqrt(square / depth + 1e-06)
    token = lax.broadcasted_iota(jnp.int32, (width, 1), 0).astype(F32)
    lane = lax.broadcasted_iota(jnp.int32, (1, LANES), 1)
    pooled = before[1][...] if before else jnp.zeros((1, LANES), F32)
    for slot, row in zip(found, here):
        count_one = base_ref[4, pl.ds(slot, 1), 0:1]
        is_first = token < count_one
        part = score[row, :]
        sum_one = jnp.sum(jnp.where(is_first, part, 0.0), axis=0, keepdims=True)
        sum_two = jnp.sum(jnp.where(is_first, 0.0, part), axis=0, keepdims=True)
        pooled = jnp.where(lane == 2 * slot, sum_one / count_one, pooled)
        pooled = jnp.where(lane == 2 * slot + 1, sum_two / (width - count_one), pooled)
    pooled_ref[...] = pooled[:, : pooled_ref.shape[1]]
    for write in writes:
        write.wait()


def call(kernel, out, ins, scratch=(), work=1, **kwargs):
    return pl.pallas_call(
        kernel,
        out_shape=out,
        in_specs=ins,
        scratch_shapes=list(scratch),
        compiler_params=pltpu.CompilerParams(vmem_limit_bytes=LIMIT),
        cost_estimate=pl.CostEstimate(
            flops=int(work * 1e9), bytes_accessed=0, transcendentals=0
        ),
        **kwargs,
    )


def in_hbm(*arrays):
    return [pltpu.with_memory_space_constraint(jnp.asarray(a), pltpu.HBM) for a in arrays]


def partner(value, axis, k):
    count = lax.axis_size(axis)
    return lax.ppermute(value, axis, [(i, i ^ k) for i in range(count)])


def hop(value, even, odd):
    heads, blocks = lax.axis_size("head"), lax.axis_size("blk")
    pairs = []
    for h in range(heads):
        for b in range(blocks):
            pairs.append((h * blocks + b, (h ^ (odd if b % 2 else even)) * blocks + b))
    return lax.ppermute(value, ("head", "blk"), pairs)


def spread_merge(backs, own, pick, slots, bpq):
    cols = backs[0].shape[0] - EXTRA
    width = backs[0].shape[1] // 2
    heads = cols // DH
    parts = jnp.stack(backs).reshape(len(backs), cols + EXTRA, 2, width)
    parts = parts.transpose(0, 2, 1, 3).reshape(2 * len(backs), cols + EXTRA, width)
    order = jnp.argsort(pick, stable=True)
    parts = jnp.take(parts, order, axis=0).reshape(slots, bpq, cols + EXTRA, width)
    stats = parts[:, :, cols : cols + 3 * heads].astype(F32)
    stats = stats.reshape(slots, bpq, 3, heads, width).sum(axis=2)
    stats = jnp.concatenate([stats, own[:, None, cols : cols + heads]], axis=1)
    weight = jnp.exp(stats - jnp.max(stats, axis=1, keepdims=True))
    weight = weight / jnp.sum(weight, axis=1, keepdims=True)
    values = jnp.concatenate([parts[:, :, :cols].astype(F32), own[:, None, :cols]], axis=1)
    values = values.reshape(slots, bpq + 1, heads, DH, width)
    mixed = jnp.sum(values * weight[:, :, :, None, :], axis=1).reshape(slots, cols, width)
    mixed = mixed.transpose(0, 2, 1).astype(BF)
    return [mixed[2 * k : 2 * k + 2].reshape(2 * width, cols) for k in range(slots // 2)]


def body(
    doc_x, doc_seg, doc_query, doc_var, query_len, block_perm, cache_k, cache_v, cache_var,
    w_query, w_key, w_value, w_out, var_bias, norm_gain, readout,
):
    rows, depth = doc_x.shape
    cols = w_query.shape[1]
    blocks = lax.axis_size("blk")
    bpq = blocks // QUERIES
    slots = QUERIES
    width = rows // slots
    chunks = blocks // 2
    order = [0, 2, 3, 1] + list(range(4, chunks))
    cache_rows = cache_k.shape[0]
    seg = doc_seg.reshape(slots, width)
    var = doc_var.reshape(slots, width)
    table = np.concatenate(offset_tables(width), axis=0)
    cache_var = cache_var.reshape(cache_rows // LANES, LANES)
    sds = jax.ShapeDtypeStruct
    i32 = jnp.int32
    chunk_shape = sds((2 * width + EXTRA, cols), BF)
    base_shape = sds((5, slots, width), F32)

    w_first = hop(w_out, 1, 2)

    pick, base, usable, packed, *queries = call(
        functools.partial(query_kernel, bpq, order),
        [
            sds((blocks,), i32), base_shape, sds((8, width), i32),
            sds((2 * cache_rows + EXTRA, cols), BF),
        ]
        + [chunk_shape] * chunks,
        [HBM] * 11,
        [pltpu.SMEM(ref.shape, i32) for ref in (doc_query, query_len, block_perm)]
        + [pltpu.VMEM(ref.shape, i32) for ref in (seg, var)]
        + [pltpu.VMEM(table.shape, F32), pltpu.VMEM(cache_var.shape, i32)]
        + [pltpu.VMEM(ref.shape, BF) for ref in (doc_x, w_query, cache_v)]
        + [pltpu.VMEM((rows, cols), F32), DMA((11,))],
        out_specs=[SMEM] + [VMEM] * (chunks + 3),
        work=3.5,
        name="query",
    )(
        *in_hbm(
            doc_query, query_len, block_perm, seg, var, table, cache_var, doc_x, w_query,
            cache_v, cache_k,
        )
    )

    asked = [queries[0]] + [partner(queries[k], "blk", 2 * order[k]) for k in range(1, chunks)]
    packed_other = partner(packed, "blk", 1)

    if bpq == 1:
        home = pick
        home_queries = queries
    else:
        home = jnp.arange(slots, dtype=i32)
        every = jnp.stack([q[: 2 * width] for q in queries]).reshape(blocks, width, cols)
        every = jnp.take(every, jnp.argsort(pick, stable=True)[::bpq], axis=0)
        home_queries = [
            every[2 * k : 2 * k + 2].reshape(2 * width, cols) for k in range(slots // 2)
        ]

    own, x_home, w_copy = call(
        own_kernel,
        [sds((slots, cols + 8, width), F32), sds((rows, depth), BF), sds(w_out.shape, BF)],
        [ANY] + [VMEM] * (8 + len(home_queries)),
        [
            pltpu.VMEM((rows, cols), F32), pltpu.VMEM((rows, cols), F32),
            pltpu.SMEM(home.shape, i32), DMA,
        ],
        out_specs=[VMEM] * 3,
        work=4.0,
        name="own_documents",
    )(home, var_bias, doc_x, w_key, w_value, var, table, base, *home_queries, w_first)

    w_second = partner(w_copy, "blk", 1)
    w_third = hop(w_copy, 2, 1)
    parts = []
    for k, query in enumerate(asked):
        after = [parts[-1] if parts else own]
        part = call(
            cache_kernel,
            chunk_shape,
            [VMEM] * 5 + [ANY] * len(after),
            out_specs=VMEM,
            work=1.5,
            name="cache_part",
        )(usable, var_bias, query, packed, packed_other, *after)
        parts.append(part)
    backs = [parts[0]] + [partner(parts[k], "blk", 2 * order[k]) for k in range(1, chunks)]

    groups = GROUPS
    if bpq == 1:
        attended = []
        for group in groups:
            after = attended[-1:] or [parts[-1], w_second, w_third]
            attended.append(
                call(
                    functools.partial(merge_kernel, [2 * k for k in group]),
                    sds((2 * width * len(group), cols), BF),
                    [VMEM] * (len(group) + 1) + [ANY] * len(after),
                    out_specs=VMEM,
                    work=20 if attended else 0.2,
                    name="merge",
                )(own, *[backs[k] for k in group], *after)
            )
    else:
        attended = spread_merge(backs, own, pick, slots, bpq)
        attended = [jnp.concatenate([attended[k] for k in group]) for group in groups]

    gain, read = norm_gain.reshape(1, depth), readout.reshape(1, depth)
    chained = []
    for group, own_part in zip(groups, attended):
        near = hop(own_part, 1, 2)
        atts = [own_part, near, hop(own_part, 2, 1), hop(near, 2, 1)]
        places = 2 * len(group)
        last = group is groups[-1]
        chained = call(
            functools.partial(output_kernel, [2 * k for k in group]),
            [sds((rows, cols), F32), sds((1, 2 * slots if last else LANES), F32)],
            [ANY] + [VMEM] * 12 + [HBM, VMEM][: len(chained)],
            [
                pltpu.VMEM((1, depth), F32), pltpu.VMEM((places * width, cols), F32),
                pltpu.SMEM(home.shape, i32), DMA((places + 1,)),
            ],
            out_specs=[HBM, VMEM],
            input_output_aliases={13: 0} if chained else {},
            work=2.5,
            name="output",
        )(home, *atts, w_out, w_first, w_second, w_third, x_home, base, gain, read, *chained)
    update, pooled = chained
    return (update, pooled.reshape(2 * slots))


def solution(mesh):
    return jax.shard_map(
        body,
        mesh=mesh,
        in_specs=(
            P("blk", None), P("blk"), P(), P("blk"), P(), P(), P("blk", "head"),
            P("blk", "head"), P("blk"), P(None, "head"), P(None, "head"), P(None, "head"),
            P("head", None), P(None, "head"), P(), P(),
        ),
        out_specs=(P("blk", "head"), P("blk")),
        check_vma=False,
    )
```

```python
import functools

import jax
import jax.numpy as jnp
import numpy as np
from jax import lax
from jax.experimental import pallas as pl
from jax.experimental.pallas import tpu as pltpu
from jax.sharding import PartitionSpec as P

DH = 64
QUERIES = 8
LANES = 128
EXTRA = 16
NEVER = -1e30
BF = jnp.bfloat16
F32 = jnp.float32
VMEM = pl.BlockSpec(memory_space=pltpu.VMEM)
SMEM = pl.BlockSpec(memory_space=pltpu.SMEM)
HBM = pl.BlockSpec(memory_space=pltpu.HBM)
ANY = pl.BlockSpec(memory_space=pl.ANY)
DMA = pltpu.SemaphoreType.DMA
LIMIT = 32 * 1024 * 1024


def offset_tables(slot_rows):
    half = DH // 2
    freq = (10000.0 ** (-np.arange(half, dtype=np.float64) / half)).astype(np.float32)
    lane_freq = np.tile(freq, LANES // half)
    angles = np.arange(slot_rows, dtype=np.float64)[:, None] * lane_freq[None, :].astype(np.float64)
    sign = np.where(np.arange(LANES) % DH < half, -1.0, 1.0).astype(np.float32)
    rows = np.zeros((8, LANES), np.float32)
    rows[0] = lane_freq
    rows[1] = sign
    return np.cos(angles).astype(np.float32), np.sin(angles).astype(np.float32), rows


def dot(a, b):
    return jnp.dot(a, b, preferred_element_type=F32)


def dot_t(a, b):
    return lax.dot_general(a, b, (((1,), (1,)), ((), ())), preferred_element_type=F32)


def slot_of(p, doc_query, block_perm, slots, bpq):
    blk = lax.axis_index("blk")
    wanted = block_perm[blk ^ p] // bpq
    slot = jnp.int32(0)
    for j in range(slots):
        slot = slot + jnp.where(doc_query[blk * 2 * slots + 2 * j] == wanted, j, 0)
    return slot


def start_tables(doc_query, query_len, seg_ref, rows_ref, base_ref):
    slots, width = seg_ref.shape
    blk = lax.axis_index("blk")
    row = lax.broadcasted_iota(jnp.int32, (slots, width), 0)
    length = jnp.zeros((slots, width), F32)
    for j in range(slots):
        value = query_len[doc_query[blk * 2 * slots + 2 * j]].astype(F32)
        length = jnp.where(row == j, value, length)
    second = (seg_ref[...] & 1).astype(F32)
    count = width - jnp.sum(second, axis=1, keepdims=True)
    count = jnp.broadcast_to(count, (slots, width))
    freq = rows_ref[0:1, :]
    one, two = length * freq, (length - count) * freq
    base_ref[0] = jnp.cos(one)
    base_ref[1] = jnp.sin(one)
    base_ref[2] = jnp.cos(two)
    base_ref[3] = jnp.sin(two)
    base_ref[4] = count


def slot_tables(slot, base_ref, cos_ref, sin_ref, rows_ref):
    shape = cos_ref.shape
    rows = [base_ref[i, pl.ds(slot, 1), :] for i in range(5)]
    token = lax.broadcasted_iota(jnp.int32, shape, 0).astype(F32)
    first = token < rows[4]
    base_cos = jnp.where(first, rows[0], rows[2])
    base_sin = jnp.where(first, rows[1], rows[3])
    off_cos, off_sin = cos_ref[...], sin_ref[...]
    cos = base_cos * off_cos - base_sin * off_sin
    sin = (base_sin * off_cos + base_cos * off_sin) * rows_ref[1:2, :]
    return cos, sin


def turn(value, cos, sin):
    lane = lax.broadcasted_iota(jnp.int32, cos.shape, 1)
    low = lane % DH < DH // 2
    parts = []
    for at in range(0, value.shape[1], LANES):
        part = value[:, at : at + LANES]
        other = jnp.where(
            low, pltpu.roll(part, LANES - DH // 2, 1), pltpu.roll(part, DH // 2, 1)
        )
        parts.append(part * cos + other * sin)
    return jnp.concatenate(parts, axis=1)


def copies(sources, targets, sems):
    moves = [
        pltpu.make_async_copy(source, target, sems.at[i])
        for i, (source, target) in enumerate(zip(sources, targets))
    ]
    for move in moves:
        move.start()
    return moves


def query_kernel(bpq, order, *refs):
    chunks = len(order)
    sources, refs = refs[:11], refs[11:]
    pick_ref, base_ref, usable_ref, packed_ref = refs[:4]
    q_refs, refs = refs[4 : 4 + chunks], refs[4 + chunks :]
    targets, (y_ref, sems) = list(refs[:10]), refs[10:]
    rows, cols = sources[10].shape
    moves = copies(sources, targets + [packed_ref.at[0:rows]], sems)
    doc_query, query_len, block_perm, seg_ref, var_ref, table_ref, key_var_ref = targets[:7]
    x_ref, w_ref, v_ref = targets[7:]
    slots, width = seg_ref.shape
    cos_ref, sin_ref = table_ref.at[0:width], table_ref.at[width : 2 * width]
    rows_ref = table_ref.at[2 * width :]
    for move in moves[:7]:
        move.wait()
    start_tables(doc_query, query_len, seg_ref, rows_ref, base_ref)
    row = lax.broadcasted_iota(jnp.int32, usable_ref.shape, 0)
    usable = jnp.zeros(usable_ref.shape, jnp.int32)
    for j in range(2):
        block = block_perm[lax.axis_index("blk") ^ j]
        here = query_len[block // bpq] - block % bpq * rows
        usable = jnp.where(row == j, here, usable)
    usable_ref[...] = usable
    parts = rows // LANES
    key_var = key_var_ref[...].astype(F32)
    key_var = jnp.concatenate([key_var, jnp.zeros((EXTRA - parts, LANES), F32)], axis=0)
    packed_ref[2 * rows :, :] = jnp.concatenate([key_var, key_var], axis=1).astype(BF)
    for move in moves[7:9]:
        move.wait()
    y_ref[...] = dot(x_ref[...], w_ref[...])
    moves[9].wait()
    for i in range(rows // cols):
        block = v_ref[i * cols : (i + 1) * cols, :].astype(F32)
        packed_ref[rows + i * cols : rows + (i + 1) * cols, :] = block.T.astype(BF)
    for k, q_ref in enumerate(q_refs):
        for j in range(2):
            slot = slot_of(2 * order[k] + j, doc_query, block_perm, slots, bpq)
            pick_ref[2 * k + j] = slot
            cos, sin = slot_tables(slot, base_ref, cos_ref, sin_ref, rows_ref)
            at = pl.ds(pl.multiple_of(slot * width, width), width)
            turned = turn(y_ref[at, :], cos, sin)
            q_ref[j * width : (j + 1) * width, :] = (turned * 0.125).astype(BF)
            var = var_ref[pl.ds(slot, 1), :].astype(F32)
            q_ref[2 * width :, j * width : (j + 1) * width] = jnp.broadcast_to(
                var, (EXTRA, width)
            ).astype(BF)
    moves[10].wait()


def by_head(query):
    lane = lax.broadcasted_iota(jnp.int32, query.shape, 1) // DH
    heads = query.shape[1] // DH
    return jnp.concatenate(
        [jnp.where(lane == h, query, jnp.zeros_like(query)) for h in range(heads)], axis=0
    )


def fold(value, op):
    while value.shape[0] > 8:
        half = value.shape[0] // 2
        value = op(value[:half], value[half:])
    return value


def attend(scores, same, allowed, bias_ref, values, out_ref, at):
    width = same.shape[1]
    stats = []
    for h in range(scores.shape[1] // width):
        part = scores[:, h * width : (h + 1) * width]
        part = part + jnp.where(same, bias_ref[0:1, h : h + 1], bias_ref[1:2, h : h + 1])
        part = jnp.where(allowed, part, NEVER)
        peak = jnp.max(fold(part, jnp.maximum), axis=0, keepdims=True)
        weight = jnp.exp(part - peak)
        total = jnp.sum(fold(weight, jnp.add), axis=0, keepdims=True)
        weight = weight.astype(BF)
        mixed = None
        key = 0
        for value in values:
            keys = value.shape[1]
            term = dot(value[h * DH : (h + 1) * DH, :], weight[key : key + keys, :])
            mixed = term if mixed is None else mixed + term
            key += keys
        mixed = mixed * (1.0 / total)
        out_ref[h * DH : (h + 1) * DH, at] = mixed.astype(out_ref.dtype)
        stats.append(peak + jnp.log(total))
    return stats


def cache_kernel(usable_ref, bias_ref, q_ref, own_ref, other_ref, *refs):
    out_ref = refs[-1]
    width = q_ref.shape[0] // 2 - EXTRA // 2
    cols = q_ref.shape[1]
    rows = (own_ref.shape[0] - EXTRA) // 2
    for j, ref in enumerate((own_ref, other_ref)):
        var = ref[2 * rows :, 0:LANES].astype(F32)
        var = jnp.concatenate([var, jnp.zeros((LANES - EXTRA, LANES), F32)], axis=0).T
        key_var = jnp.concatenate(
            [jnp.broadcast_to(var[:, i : i + 1], (LANES, width)) for i in range(rows // LANES)],
            axis=0,
        )
        tok_var = q_ref[2 * width :, j * width : (j + 1) * width].astype(F32)[0:1, :]
        same = key_var == tok_var
        allowed = lax.broadcasted_iota(jnp.int32, (rows, width), 0) < usable_ref[j : j + 1, :]
        scores = dot_t(ref[0:rows, :], by_head(q_ref[j * width : (j + 1) * width, :]))
        values = [ref[rows + i * cols : rows + (i + 1) * cols, :] for i in range(rows // cols)]
        at = slice(j * width, (j + 1) * width)
        stats = attend(scores, same, allowed, bias_ref, values, out_ref, at)
        full = jnp.concatenate(stats, axis=0)
        high = full.astype(BF).astype(F32)
        middle = (full - high).astype(BF).astype(F32)
        low = full - high - middle
        pad = jnp.zeros((EXTRA - 3 * len(stats), width), F32)
        out_ref[cols:, at] = jnp.concatenate([high, middle, low, pad], axis=0).astype(BF)


def own_kernel(
    home_any, bias_ref, x_ref, wk_ref, wv_ref, var_ref, table_ref, base_ref,
    *refs
):
    w_ref, out_ref, x_part_ref, count_ref, w_copy_ref, k_ref, v_ref, home_ref, sem = refs[-9:]
    q_refs = refs[:-9]
    part = x_part_ref.shape[0] // var_ref.shape[0]
    part_start = lax.axis_index("head") * part
    w_copy_ref[...] = w_ref[...]
    slots, width = var_ref.shape
    cols = wk_ref.shape[1]
    home_move = pltpu.make_async_copy(home_any, home_ref, sem)
    home_move.start()
    cos_ref, sin_ref = table_ref.at[0:width], table_ref.at[width : 2 * width]
    rows_ref = table_ref.at[2 * width :]
    k_ref[...] = dot(x_ref[...], wk_ref[...])
    v_ref[...] = dot(x_ref[...], wv_ref[...])
    home_move.wait()
    for n in range(slots):
        slot = home_ref[n]
        cos, sin = slot_tables(slot, base_ref, cos_ref, sin_ref, rows_ref)
        at = pl.ds(pl.multiple_of(slot * width, width), width)
        part_at = pl.ds(pl.multiple_of(slot * width + part_start, part), part)
        x_part_ref[n * part : (n + 1) * part, :] = x_ref[part_at, :]
        key = turn(k_ref[at, :], cos, sin).astype(BF)
        value = v_ref[at, :].T.astype(BF)
        query = q_refs[n // 2][n % 2 * width : (n % 2 + 1) * width, :]
        scores = dot_t(key, by_head(query))
        var = jnp.broadcast_to(var_ref[pl.ds(slot, 1), :].astype(F32), (width, width))
        same = var.T == var
        count = base_ref[4, pl.ds(slot, 1), :]
        count_ref[n : n + 1, :] = count
        key_second = lax.broadcasted_iota(jnp.int32, (width, width), 0).astype(F32) >= count
        tok_second = lax.broadcasted_iota(jnp.int32, (width, width), 1).astype(F32) >= count
        allowed = jnp.logical_not(jnp.logical_xor(key_second, tok_second))
        part_ref = out_ref.at[n]
        stats = attend(scores, same, allowed, bias_ref, [value], part_ref, slice(None))
        stats = jnp.concatenate(stats + [jnp.zeros((8 - len(stats), width), F32)], axis=0)
        part_ref[cols:, :] = stats


def distances():
    core = lax.axis_index("blk") % 2
    return [0, 1 + core, 2 - core, 3]


def merge(first, got_ref, own_ref, out_ref, start):
    cols = got_ref.shape[0] - EXTRA
    heads = cols // DH
    width = got_ref.shape[1] // 2
    for j in range(2):
        at = slice(j * width, (j + 1) * width)
        stats = got_ref[cols:, at].astype(F32)
        there = stats[0:heads] + stats[heads : 2 * heads] + stats[2 * heads : 3 * heads]
        here = own_ref[first + j, cols : cols + heads, :]
        peak = jnp.maximum(there, here)
        there, here = jnp.exp(there - peak), jnp.exp(here - peak)
        inverse = 1.0 / (there + here)
        there, here = there * inverse, here * inverse
        parts = []
        for h in range(heads):
            row = slice(h * DH, (h + 1) * DH)
            parts.append(
                got_ref[row, at].astype(F32) * there[h : h + 1]
                + own_ref[first + j, row, :] * here[h : h + 1]
            )
        to = slice(start + j * width, start + (j + 1) * width)
        out_ref[to, :] = jnp.concatenate(parts, axis=0).T.astype(BF)


def merge_kernel(chunk, own_ref, got_ref, *refs):
    out_ref = refs[-1]
    merge(2 * chunk, got_ref, own_ref, out_ref, 0)


def last_merge_kernel(chunk, earlier, own_ref, got_ref, *refs):
    att_refs = [*refs[:earlier], refs[-1]]
    out_refs = refs[-5:-1]
    merge(2 * chunk, got_ref, own_ref, refs[-1], 0)
    slots = 2 * len(att_refs)
    width = refs[-1].shape[0] // 2
    part = out_refs[0].shape[0] // slots
    head = lax.axis_index("head")
    for distance, out_ref in zip(distances(), out_refs):
        for n in range(slots):
            start = pl.multiple_of(n % 2 * width + (head ^ distance) * part, part)
            out_ref[n * part : (n + 1) * part, :] = att_refs[n // 2][pl.ds(start, part), :]


def output_kernel(*refs):
    att_halves, refs = (refs[0:4], refs[4:8]), refs[8:]
    w_refs = refs[:4]
    x_ref, count_ref, gain_ref, read_ref = refs[4:8]
    mine_ref, sums_ref = refs[8:10]
    send_refs, gr_ref, att_refs = refs[10:13], refs[13], refs[14:]
    for first_ref, second_ref, att_ref in zip(*att_halves, att_refs):
        att_ref[0 : first_ref.shape[0], :] = first_ref[...]
        att_ref[first_ref.shape[0] :, :] = second_ref[...]
    tokens, cols = att_refs[0].shape
    depth = w_refs[0].shape[1]
    slots = count_ref.shape[0]
    part = tokens // slots
    gr_ref[...] = gain_ref[...] * read_ref[...]
    head = lax.axis_index("head")
    square = jnp.zeros((tokens, LANES), F32)
    weighted = jnp.zeros((tokens, LANES), F32)
    for c, distance in enumerate(distances()):
        at = pl.ds(pl.multiple_of((head ^ distance) * cols, cols), cols)
        total = dot(att_refs[0][...], w_refs[0][:, at])
        for att_ref, w_ref in zip(att_refs[1:], w_refs[1:]):
            total = total + dot(att_ref[...], w_ref[:, at])
        if c == 0:
            mine_ref[...] = total
        else:
            send_refs[c - 1][0:tokens, :] = total.astype(BF)
        hidden = x_ref[:, at].astype(F32) + total
        scaled = hidden * gr_ref[:, at]
        hidden = hidden * hidden
        for lane in range(0, cols, LANES):
            square = square + hidden[:, lane : lane + LANES]
            weighted = weighted + scaled[:, lane : lane + LANES]
    square = jnp.sum(square, axis=1, keepdims=True)
    weighted = jnp.sum(weighted, axis=1, keepdims=True)
    score = weighted * lax.rsqrt(square / depth + 1e-06)
    token = lax.broadcasted_iota(jnp.int32, (part, 1), 0) + head * part
    lane = lax.broadcasted_iota(jnp.int32, (1, LANES), 1)
    sums = jnp.zeros((1, LANES), F32)
    for n in range(slots):
        is_first = token.astype(F32) < count_ref[n : n + 1, 0:1]
        piece = score[n * part : (n + 1) * part, :]
        sum_one = jnp.sum(jnp.where(is_first, piece, 0.0), axis=0, keepdims=True)
        sum_two = jnp.sum(jnp.where(is_first, 0.0, piece), axis=0, keepdims=True)
        sums = jnp.where(lane == 2 * n, sum_one, sums)
        sums = jnp.where(lane == 2 * n + 1, sum_two, sums)
    sums_ref[...] = jnp.broadcast_to(sums, sums_ref.shape)
    high = sums.astype(BF).astype(F32)
    middle = (sums - high).astype(BF).astype(F32)
    low = sums - high - middle
    block = jnp.concatenate([high, middle, low, jnp.zeros((EXTRA - 3, LANES), F32)], axis=0)
    block = jnp.concatenate([block] * (cols // LANES), axis=1).astype(BF)
    for send_ref in send_refs:
        send_ref[tokens:, :] = block


def place_kernel(home_any, mine_ref, *refs):
    got_refs = refs[:3]
    sums_ref, count_ref, update_hbm, pooled_ref, stage_ref, home_ref, sems = refs[3:]
    slots = count_ref.shape[0]
    home_move = pltpu.make_async_copy(home_any, home_ref, sems.at[slots])
    home_move.start()
    tokens = mine_ref.shape[0]
    part = tokens // slots
    width = stage_ref.shape[0] // slots
    head = lax.axis_index("head")
    for n in range(slots):
        for distance, ref in zip(distances(), (mine_ref, *got_refs)):
            start = pl.multiple_of(n * width + (head ^ distance) * part, part)
            stage_ref[pl.ds(start, part), :] = ref[n * part : (n + 1) * part, :].astype(F32)
    home_move.wait()
    moves = []
    for n in range(slots):
        to = pl.ds(pl.multiple_of(home_ref[n] * width, width), width)
        move = pltpu.make_async_copy(
            stage_ref.at[n * width : (n + 1) * width], update_hbm.at[to], sems.at[n]
        )
        move.start()
        moves.append(move)
    sums = sums_ref[0:1, :]
    for ref in got_refs:
        block = ref[tokens:, 0:LANES].astype(F32)
        sums = sums + (block[0:1] + block[1:2] + block[2:3])
    lane = lax.broadcasted_iota(jnp.int32, (1, LANES), 1)
    pooled = jnp.zeros((1, LANES), F32)
    for n in range(slots):
        slot, count = home_ref[n], count_ref[n : n + 1, 0:1]
        pooled = jnp.where(lane == 2 * slot, sums[:, 2 * n : 2 * n + 1] / count, pooled)
        pooled = jnp.where(
            lane == 2 * slot + 1, sums[:, 2 * n + 1 : 2 * n + 2] / (width - count), pooled
        )
    pooled_ref[...] = pooled[:, : pooled_ref.shape[1]]
    for move in moves:
        move.wait()


def call(kernel, out, ins, scratch=(), work=1, **kwargs):
    return pl.pallas_call(
        kernel,
        out_shape=out,
        in_specs=ins,
        scratch_shapes=list(scratch),
        compiler_params=pltpu.CompilerParams(vmem_limit_bytes=LIMIT),
        cost_estimate=pl.CostEstimate(
            flops=int(work * 1e9), bytes_accessed=0, transcendentals=0
        ),
        **kwargs,
    )


def in_hbm(*arrays):
    return [pltpu.with_memory_space_constraint(jnp.asarray(a), pltpu.HBM) for a in arrays]


def partner(value, axis, k):
    count = lax.axis_size(axis)
    return lax.ppermute(value, axis, [(i, i ^ k) for i in range(count)])


def hop(value, even, odd):
    heads, blocks = lax.axis_size("head"), lax.axis_size("blk")
    pairs = []
    for h in range(heads):
        for b in range(blocks):
            pairs.append((h * blocks + b, (h ^ (odd if b % 2 else even)) * blocks + b))
    return lax.ppermute(value, ("head", "blk"), pairs)


def spread_merge(backs, own, pick, slots, bpq):
    cols = backs[0].shape[0] - EXTRA
    width = backs[0].shape[1] // 2
    heads = cols // DH
    parts = jnp.stack(backs).reshape(len(backs), cols + EXTRA, 2, width)
    parts = parts.transpose(0, 2, 1, 3).reshape(2 * len(backs), cols + EXTRA, width)
    order = jnp.argsort(pick, stable=True)
    parts = jnp.take(parts, order, axis=0).reshape(slots, bpq, cols + EXTRA, width)
    stats = parts[:, :, cols : cols + 3 * heads].astype(F32)
    stats = stats.reshape(slots, bpq, 3, heads, width).sum(axis=2)
    stats = jnp.concatenate([stats, own[:, None, cols : cols + heads]], axis=1)
    weight = jnp.exp(stats - jnp.max(stats, axis=1, keepdims=True))
    weight = weight / jnp.sum(weight, axis=1, keepdims=True)
    values = jnp.concatenate([parts[:, :, :cols].astype(F32), own[:, None, :cols]], axis=1)
    values = values.reshape(slots, bpq + 1, heads, DH, width)
    mixed = jnp.sum(values * weight[:, :, :, None, :], axis=1).reshape(slots, cols, width)
    mixed = mixed.transpose(0, 2, 1).astype(BF)
    return [mixed[2 * k : 2 * k + 2].reshape(2 * width, cols) for k in range(slots // 2)]


def body(
    doc_x, doc_seg, doc_query, doc_var, query_len, block_perm, cache_k, cache_v, cache_var,
    w_query, w_key, w_value, w_out, var_bias, norm_gain, readout,
):
    rows, depth = doc_x.shape
    cols = w_query.shape[1]
    blocks = lax.axis_size("blk")
    heads = lax.axis_size("head")
    bpq = blocks // QUERIES
    slots = QUERIES
    width = rows // slots
    chunks = blocks // 2
    order = list(range(chunks))
    cache_rows = cache_k.shape[0]
    seg = doc_seg.reshape(slots, width)
    var = doc_var.reshape(slots, width)
    table = np.concatenate(offset_tables(width), axis=0)
    cache_var = cache_var.reshape(cache_rows // LANES, LANES)
    sds = jax.ShapeDtypeStruct
    i32 = jnp.int32
    chunk_shape = sds((2 * width + EXTRA, cols), BF)
    base_shape = sds((5, slots, width), F32)

    w_first = hop(w_out, 1, 2)

    pick, base, usable, packed, *queries = call(
        functools.partial(query_kernel, bpq, order),
        [
            sds((blocks,), i32), base_shape, sds((8, width), i32),
            sds((2 * cache_rows + EXTRA, cols), BF),
        ]
        + [chunk_shape] * chunks,
        [HBM] * 11,
        [pltpu.SMEM(ref.shape, i32) for ref in (doc_query, query_len, block_perm)]
        + [pltpu.VMEM(ref.shape, i32) for ref in (seg, var)]
        + [pltpu.VMEM(table.shape, F32), pltpu.VMEM(cache_var.shape, i32)]
        + [pltpu.VMEM(ref.shape, BF) for ref in (doc_x, w_query, cache_v)]
        + [pltpu.VMEM((rows, cols), F32), DMA((11,))],
        out_specs=[SMEM] + [VMEM] * (chunks + 3),
        work=3.5,
        name="query",
    )(
        *in_hbm(
            doc_query, query_len, block_perm, seg, var, table, cache_var, doc_x, w_query,
            cache_v, cache_k,
        )
    )

    asked = [queries[0]] + [partner(queries[k], "blk", 2 * order[k]) for k in range(1, chunks)]
    packed_other = partner(packed, "blk", 1)

    if bpq == 1:
        home = pick
        home_queries = queries
    else:
        home = jnp.arange(slots, dtype=i32)
        every = jnp.stack([q[: 2 * width] for q in queries]).reshape(blocks, width, cols)
        every = jnp.take(every, jnp.argsort(pick, stable=True)[::bpq], axis=0)
        home_queries = [
            every[2 * k : 2 * k + 2].reshape(2 * width, cols) for k in range(slots // 2)
        ]

    own, x_part, count, w_copy = call(
        own_kernel,
        [
            sds((slots, cols + 8, width), F32), sds((rows // heads, depth), BF),
            sds((slots, width), F32), sds(w_out.shape, BF),
        ],
        [ANY] + [VMEM] * (8 + len(home_queries)),
        [
            pltpu.VMEM((rows, cols), F32), pltpu.VMEM((rows, cols), F32),
            pltpu.SMEM(home.shape, i32), DMA,
        ],
        out_specs=[VMEM] * 4,
        work=4.0,
        name="own_documents",
    )(home, var_bias, doc_x, w_key, w_value, var, table, base, *home_queries, w_first)

    w_second = partner(w_copy, "blk", 1)
    w_third = hop(w_copy, 2, 1)
    parts = []
    for k, query in enumerate(asked):
        after = [parts[-1] if parts else own]
        part = call(
            cache_kernel,
            chunk_shape,
            [VMEM] * 5 + [ANY] * len(after),
            out_specs=VMEM,
            work=1.5,
            name="cache_part",
        )(usable, var_bias, query, packed, packed_other, *after)
        parts.append(part)
    backs = [parts[0]] + [partner(parts[k], "blk", 2 * order[k]) for k in range(1, chunks)]

    def spread(a, b, c):
        return [hop(a, 1, 2), hop(b, 2, 1), partner(c, "head", 3)]

    part_shape = sds((rows // heads // 2, cols), BF)
    halves = []
    if bpq == 1:
        chunk_att = sds((2 * width, cols), BF)
        after, waiting = [parts[-1], w_second, w_third], []
        for group in (range(chunks // 2), range(chunks // 2, chunks)):
            attended = []
            for k in group[:-1]:
                attended.append(
                    call(
                        functools.partial(merge_kernel, k),
                        chunk_att,
                        [VMEM] * 2 + [ANY] * len(after),
                        out_specs=VMEM,
                        work=20 if halves else 0.2,
                        name="merge",
                    )(own, backs[k], *after)
                )
                after = attended[-1:]
            pieces = call(
                functools.partial(last_merge_kernel, group[-1], len(attended)),
                [part_shape] * 4,
                [VMEM] * (2 + len(attended)) + [ANY] * len(after + waiting),
                [pltpu.VMEM(chunk_att.shape, BF)],
                out_specs=[VMEM] * 4,
                work=20 if halves else 0.2,
                name="last_merge",
            )(own, backs[group[-1]], *attended, *after, *waiting)
            halves.append([pieces[0], *spread(*pieces[1:])])
            after, waiting = pieces[:1], halves[-1][1:]
    else:
        attended = spread_merge(backs, own, pick, slots, bpq)
        attended = jnp.concatenate(attended).reshape(slots, width, cols)
        head, part = lax.axis_index("head"), width // heads
        pieces = [
            lax.dynamic_slice_in_dim(attended, (head ^ distance) * part, part, 1)
            for distance in distances()
        ]
        pieces = [piece.reshape(2, *part_shape.shape) for piece in pieces]
        halves = [[piece[i] for piece in pieces] for i in range(2)]
        halves = [[piece, *spread(*others)] for piece, *others in halves]

    gain, read = norm_gain.reshape(1, depth), readout.reshape(1, depth)
    send_shape = sds((rows // heads + EXTRA, cols), BF)
    mine, sums, *sends = call(
        output_kernel,
        [sds((rows // heads, cols), F32), sds((8, LANES), F32)] + [send_shape] * 3,
        [VMEM] * 16,
        [pltpu.VMEM((1, depth), F32)] + [pltpu.VMEM((rows // heads, cols), BF)] * 4,
        out_specs=[VMEM] * 5,
        work=2.0,
        name="output",
    )(
        *halves[0], *halves[1],
        w_out, w_first, w_second, w_third, x_part, count, gain, read,
    )
    update, pooled = call(
        place_kernel,
        [sds((rows, cols), F32), sds((1, 2 * slots), F32)],
        [ANY] + [VMEM] * 6,
        [pltpu.VMEM((rows, cols), F32), pltpu.SMEM(home.shape, i32), DMA((slots + 1,))],
        out_specs=[HBM, VMEM],
        work=1.5,
        name="place",
    )(home, mine, *spread(*sends), sums, count)
    return (update, pooled.reshape(2 * slots))


def solution(mesh):
    return jax.shard_map(
        body,
        mesh=mesh,
        in_specs=(
            P("blk", None), P("blk"), P(), P("blk"), P(), P(), P("blk", "head"),
            P("blk", "head"), P("blk"), P(None, "head"), P(None, "head"), P(None, "head"),
            P("head", None), P(None, "head"), P(), P(),
        ),
        out_specs=(P("blk", "head"), P("blk")),
        check_vma=False,
    )
```

```python
import functools

import jax
import jax.numpy as jnp
import numpy as np
from jax import lax
from jax.experimental import pallas as pl
from jax.experimental.pallas import tpu as pltpu
from jax.sharding import PartitionSpec as P

DH = 64
QUERIES = 8
LANES = 128
EXTRA = 16
NEVER = -1e30
BF = jnp.bfloat16
F32 = jnp.float32
VMEM = pl.BlockSpec(memory_space=pltpu.VMEM)
SMEM = pl.BlockSpec(memory_space=pltpu.SMEM)
HBM = pl.BlockSpec(memory_space=pltpu.HBM)
ANY = pl.BlockSpec(memory_space=pl.ANY)
DMA = pltpu.SemaphoreType.DMA
LIMIT = 32 * 1024 * 1024


def offset_tables(slot_rows):
    half = DH // 2
    freq = (10000.0 ** (-np.arange(half, dtype=np.float64) / half)).astype(np.float32)
    lane_freq = np.tile(freq, LANES // half)
    angles = np.arange(slot_rows, dtype=np.float64)[:, None] * lane_freq[None, :].astype(np.float64)
    sign = np.where(np.arange(LANES) % DH < half, -1.0, 1.0).astype(np.float32)
    rows = np.zeros((8, LANES), np.float32)
    rows[0] = lane_freq
    rows[1] = sign
    return np.cos(angles).astype(np.float32), np.sin(angles).astype(np.float32), rows


def dot(a, b):
    return jnp.dot(a, b, preferred_element_type=F32)


def dot_t(a, b):
    return lax.dot_general(a, b, (((1,), (1,)), ((), ())), preferred_element_type=F32)


def slot_of(p, doc_query, block_perm, slots, bpq):
    blk = lax.axis_index("blk")
    wanted = block_perm[blk ^ p] // bpq
    slot = jnp.int32(0)
    for j in range(slots):
        slot = slot + jnp.where(doc_query[blk * 2 * slots + 2 * j] == wanted, j, 0)
    return slot


def start_tables(doc_query, query_len, seg_ref, rows_ref, base_ref):
    slots, width = seg_ref.shape
    blk = lax.axis_index("blk")
    row = lax.broadcasted_iota(jnp.int32, (slots, width), 0)
    length = jnp.zeros((slots, width), F32)
    for j in range(slots):
        value = query_len[doc_query[blk * 2 * slots + 2 * j]].astype(F32)
        length = jnp.where(row == j, value, length)
    second = (seg_ref[...] & 1).astype(F32)
    count = width - jnp.sum(second, axis=1, keepdims=True)
    count = jnp.broadcast_to(count, (slots, width))
    freq = rows_ref[0:1, :]
    one, two = length * freq, (length - count) * freq
    base_ref[0] = jnp.cos(one)
    base_ref[1] = jnp.sin(one)
    base_ref[2] = jnp.cos(two)
    base_ref[3] = jnp.sin(two)
    base_ref[4] = count


def slot_tables(slot, base_ref, cos_ref, sin_ref, rows_ref):
    shape = cos_ref.shape
    rows = [base_ref[i, pl.ds(slot, 1), :] for i in range(5)]
    token = lax.broadcasted_iota(jnp.int32, shape, 0).astype(F32)
    first = token < rows[4]
    base_cos = jnp.where(first, rows[0], rows[2])
    base_sin = jnp.where(first, rows[1], rows[3])
    off_cos, off_sin = cos_ref[...], sin_ref[...]
    cos = base_cos * off_cos - base_sin * off_sin
    sin = (base_sin * off_cos + base_cos * off_sin) * rows_ref[1:2, :]
    return cos, sin


def turn(value, cos, sin):
    lane = lax.broadcasted_iota(jnp.int32, cos.shape, 1)
    low = lane % DH < DH // 2
    parts = []
    for at in range(0, value.shape[1], LANES):
        part = value[:, at : at + LANES]
        other = jnp.where(
            low, pltpu.roll(part, LANES - DH // 2, 1), pltpu.roll(part, DH // 2, 1)
        )
        parts.append(part * cos + other * sin)
    return jnp.concatenate(parts, axis=1)


def copies(sources, targets, sems):
    moves = [
        pltpu.make_async_copy(source, target, sems.at[i])
        for i, (source, target) in enumerate(zip(sources, targets))
    ]
    for move in moves:
        move.start()
    return moves


def query_kernel(bpq, order, *refs):
    chunks = len(order)
    sources, refs = refs[:11], refs[11:]
    pick_ref, base_ref, usable_ref, packed_ref, cos_ref, sin_ref = refs[:6]
    q_refs, refs = refs[6 : 6 + chunks], refs[6 + chunks :]
    targets, (y_ref, sems) = list(refs[:10]), refs[10:]
    rows, cols = sources[8].shape
    moves = copies(sources, targets[:8] + [packed_ref.at[0:rows]] + targets[8:], sems)
    doc_query, query_len, block_perm, seg_ref, var_ref, table_ref, key_var_ref, v_ref = targets[:8]
    w_ref, x_ref = targets[8:]
    slots, width = seg_ref.shape
    for move in moves[:7]:
        move.wait()
    rows_ref = table_ref.at[2 * width :]
    start_tables(doc_query, query_len, seg_ref, rows_ref, base_ref)
    row = lax.broadcasted_iota(jnp.int32, usable_ref.shape, 0)
    usable = jnp.zeros(usable_ref.shape, jnp.int32)
    for j in range(2):
        block = block_perm[lax.axis_index("blk") ^ j]
        here = query_len[block // bpq] - block % bpq * rows
        usable = jnp.where(row == j, here, usable)
    usable_ref[...] = usable
    for slot in range(slots):
        cos, sin = slot_tables(
            slot, base_ref, table_ref.at[0:width], table_ref.at[width : 2 * width], rows_ref
        )
        cos_ref[slot * width : (slot + 1) * width, :] = cos
        sin_ref[slot * width : (slot + 1) * width, :] = sin
    found = [
        slot_of(2 * order[k] + j, doc_query, block_perm, slots, bpq)
        for k in range(chunks)
        for j in range(2)
    ]
    for p, slot in enumerate(found):
        pick_ref[p] = slot
        q_ref, j = q_refs[p // 2], p % 2
        var = var_ref[pl.ds(slot, 1), :].astype(F32)
        q_ref[2 * width :, j * width : (j + 1) * width] = jnp.broadcast_to(
            var, (EXTRA, width)
        ).astype(BF)
    parts = rows // LANES
    key_var = key_var_ref[...].astype(F32)
    key_var = jnp.concatenate([key_var, jnp.zeros((EXTRA - parts, LANES), F32)], axis=0)
    packed_ref[2 * rows :, :] = jnp.concatenate([key_var, key_var], axis=1).astype(BF)
    moves[7].wait()
    for i in range(rows // cols):
        block = v_ref[i * cols : (i + 1) * cols, :].astype(F32)
        packed_ref[rows + i * cols : rows + (i + 1) * cols, :] = block.T.astype(BF)
    for move in moves[8:]:
        move.wait()
    y_ref[...] = dot(x_ref[...], w_ref[...])
    for p, slot in enumerate(found):
        q_ref, j = q_refs[p // 2], p % 2
        at = pl.ds(pl.multiple_of(slot * width, width), width)
        turned = turn(y_ref[at, :], cos_ref[at, :], sin_ref[at, :])
        q_ref[j * width : (j + 1) * width, :] = (turned * 0.125).astype(BF)


def by_head(query):
    lane = lax.broadcasted_iota(jnp.int32, query.shape, 1) // DH
    heads = query.shape[1] // DH
    return jnp.concatenate(
        [jnp.where(lane == h, query, jnp.zeros_like(query)) for h in range(heads)], axis=0
    )


def fold(value, op):
    while value.shape[0] > 8:
        half = value.shape[0] // 2
        value = op(value[:half], value[half:])
    return value


def attend(scores, same, allowed, bias_ref, values, out_ref, at):
    width = same.shape[1]
    stats = []
    for h in range(scores.shape[1] // width):
        part = scores[:, h * width : (h + 1) * width]
        part = part + jnp.where(same, bias_ref[0:1, h : h + 1], bias_ref[1:2, h : h + 1])
        part = jnp.where(allowed, part, NEVER)
        peak = jnp.max(fold(part, jnp.maximum), axis=0, keepdims=True)
        weight = jnp.exp(part - peak)
        total = jnp.sum(fold(weight, jnp.add), axis=0, keepdims=True)
        weight = weight.astype(BF)
        mixed = None
        key = 0
        for value in values:
            keys = value.shape[1]
            term = dot(value[h * DH : (h + 1) * DH, :], weight[key : key + keys, :])
            mixed = term if mixed is None else mixed + term
            key += keys
        mixed = mixed * (1.0 / total)
        out_ref[h * DH : (h + 1) * DH, at] = mixed.astype(out_ref.dtype)
        stats.append(peak + jnp.log(total))
    return stats


def cache_kernel(usable_ref, bias_ref, q_ref, own_ref, other_ref, *refs):
    out_ref = refs[-1]
    width = q_ref.shape[0] // 2 - EXTRA // 2
    cols = q_ref.shape[1]
    rows = (own_ref.shape[0] - EXTRA) // 2
    for j, ref in enumerate((own_ref, other_ref)):
        var = ref[2 * rows :, 0:LANES].astype(F32)
        var = jnp.concatenate([var, jnp.zeros((LANES - EXTRA, LANES), F32)], axis=0).T
        key_var = jnp.concatenate(
            [jnp.broadcast_to(var[:, i : i + 1], (LANES, width)) for i in range(rows // LANES)],
            axis=0,
        )
        tok_var = q_ref[2 * width :, j * width : (j + 1) * width].astype(F32)[0:1, :]
        same = key_var == tok_var
        allowed = lax.broadcasted_iota(jnp.int32, (rows, width), 0) < usable_ref[j : j + 1, :]
        scores = dot_t(ref[0:rows, :], by_head(q_ref[j * width : (j + 1) * width, :]))
        values = [ref[rows + i * cols : rows + (i + 1) * cols, :] for i in range(rows // cols)]
        at = slice(j * width, (j + 1) * width)
        stats = attend(scores, same, allowed, bias_ref, values, out_ref, at)
        full = jnp.concatenate(stats, axis=0)
        high = full.astype(BF).astype(F32)
        middle = (full - high).astype(BF).astype(F32)
        low = full - high - middle
        pad = jnp.zeros((EXTRA - 3 * len(stats), width), F32)
        out_ref[cols:, at] = jnp.concatenate([high, middle, low, pad], axis=0).astype(BF)


def own_kernel(
    home_any, bias_ref, x_ref, wk_ref, wv_ref, var_ref, cos_ref, sin_ref, base_ref,
    *refs
):
    w_ref, out_ref, x_part_ref, count_ref, w_copy_ref, k_ref, v_ref, home_ref, sem = refs[-9:]
    q_refs = refs[:-9]
    part = x_part_ref.shape[0] // var_ref.shape[0]
    part_start = lax.axis_index("head") * part
    w_copy_ref[...] = w_ref[...]
    slots, width = var_ref.shape
    cols = wk_ref.shape[1]
    home_move = pltpu.make_async_copy(home_any, home_ref, sem)
    home_move.start()
    k_ref[...] = dot(x_ref[...], wk_ref[...])
    v_ref[...] = dot(x_ref[...], wv_ref[...])
    home_move.wait()
    for n in range(slots):
        slot = home_ref[n]
        at = pl.ds(pl.multiple_of(slot * width, width), width)
        cos, sin = cos_ref[at, :], sin_ref[at, :]
        part_at = pl.ds(pl.multiple_of(slot * width + part_start, part), part)
        x_part_ref[n * part : (n + 1) * part, :] = x_ref[part_at, :]
        key = turn(k_ref[at, :], cos, sin).astype(BF)
        value = v_ref[at, :].T.astype(BF)
        query = q_refs[n // 2][n % 2 * width : (n % 2 + 1) * width, :]
        scores = dot_t(key, by_head(query))
        var = jnp.broadcast_to(var_ref[pl.ds(slot, 1), :].astype(F32), (width, width))
        same = var.T == var
        count = base_ref[4, pl.ds(slot, 1), :]
        count_ref[n : n + 1, :] = count
        key_second = lax.broadcasted_iota(jnp.int32, (width, width), 0).astype(F32) >= count
        tok_second = lax.broadcasted_iota(jnp.int32, (width, width), 1).astype(F32) >= count
        allowed = jnp.logical_not(jnp.logical_xor(key_second, tok_second))
        part_ref = out_ref.at[n]
        stats = attend(scores, same, allowed, bias_ref, [value], part_ref, slice(None))
        stats = jnp.concatenate(stats + [jnp.zeros((8 - len(stats), width), F32)], axis=0)
        part_ref[cols:, :] = stats


def distances():
    core = lax.axis_index("blk") % 2
    return [0, 1 + core, 2 - core, 3]


def merge(first, got_ref, own_ref, out_ref, start):
    cols = got_ref.shape[0] - EXTRA
    heads = cols // DH
    width = got_ref.shape[1] // 2
    for j in range(2):
        at = slice(j * width, (j + 1) * width)
        stats = got_ref[cols:, at].astype(F32)
        there = stats[0:heads] + stats[heads : 2 * heads] + stats[2 * heads : 3 * heads]
        here = own_ref[first + j, cols : cols + heads, :]
        peak = jnp.maximum(there, here)
        there, here = jnp.exp(there - peak), jnp.exp(here - peak)
        inverse = 1.0 / (there + here)
        there, here = there * inverse, here * inverse
        parts = []
        for h in range(heads):
            row = slice(h * DH, (h + 1) * DH)
            parts.append(
                got_ref[row, at].astype(F32) * there[h : h + 1]
                + own_ref[first + j, row, :] * here[h : h + 1]
            )
        to = slice(start + j * width, start + (j + 1) * width)
        out_ref[to, :] = jnp.concatenate(parts, axis=0).T.astype(BF)


def merge_kernel(chunk, own_ref, got_ref, *refs):
    out_ref = refs[-1]
    merge(2 * chunk, got_ref, own_ref, out_ref, 0)


def last_merge_kernel(chunk, earlier, own_ref, got_ref, *refs):
    att_refs = [*refs[:earlier], refs[-1]]
    out_refs = refs[-5:-1]
    merge(2 * chunk, got_ref, own_ref, refs[-1], 0)
    slots = 2 * len(att_refs)
    width = refs[-1].shape[0] // 2
    part = out_refs[0].shape[0] // slots
    head = lax.axis_index("head")
    for distance, out_ref in zip(distances(), out_refs):
        for n in range(slots):
            start = pl.multiple_of(n % 2 * width + (head ^ distance) * part, part)
            out_ref[n * part : (n + 1) * part, :] = att_refs[n // 2][pl.ds(start, part), :]


def output_kernel(*refs):
    att_halves, refs = (refs[0:4], refs[4:8]), refs[8:]
    w_refs = refs[:4]
    x_ref, count_ref, gain_ref, read_ref = refs[4:8]
    mine_ref, sums_ref = refs[8:10]
    send_refs, gr_ref, att_refs = refs[10:13], refs[13], refs[14:]
    for first_ref, second_ref, att_ref in zip(*att_halves, att_refs):
        att_ref[0 : first_ref.shape[0], :] = first_ref[...]
        att_ref[first_ref.shape[0] :, :] = second_ref[...]
    tokens, cols = att_refs[0].shape
    depth = w_refs[0].shape[1]
    slots = count_ref.shape[0]
    part = tokens // slots
    gr_ref[...] = gain_ref[...] * read_ref[...]
    head = lax.axis_index("head")
    square = jnp.zeros((tokens, LANES), F32)
    weighted = jnp.zeros((tokens, LANES), F32)
    for c, distance in enumerate(distances()):
        at = pl.ds(pl.multiple_of((head ^ distance) * cols, cols), cols)
        total = dot(att_refs[0][...], w_refs[0][:, at])
        for att_ref, w_ref in zip(att_refs[1:], w_refs[1:]):
            total = total + dot(att_ref[...], w_ref[:, at])
        if c == 0:
            mine_ref[...] = total
        else:
            send_refs[c - 1][0:tokens, :] = total.astype(BF)
        hidden = x_ref[:, at].astype(F32) + total
        scaled = hidden * gr_ref[:, at]
        hidden = hidden * hidden
        for lane in range(0, cols, LANES):
            square = square + hidden[:, lane : lane + LANES]
            weighted = weighted + scaled[:, lane : lane + LANES]
    square = jnp.sum(square, axis=1, keepdims=True)
    weighted = jnp.sum(weighted, axis=1, keepdims=True)
    score = weighted * lax.rsqrt(square / depth + 1e-06)
    token = lax.broadcasted_iota(jnp.int32, (part, 1), 0) + head * part
    lane = lax.broadcasted_iota(jnp.int32, (1, LANES), 1)
    sums = jnp.zeros((1, LANES), F32)
    for n in range(slots):
        is_first = token.astype(F32) < count_ref[n : n + 1, 0:1]
        piece = score[n * part : (n + 1) * part, :]
        sum_one = jnp.sum(jnp.where(is_first, piece, 0.0), axis=0, keepdims=True)
        sum_two = jnp.sum(jnp.where(is_first, 0.0, piece), axis=0, keepdims=True)
        sums = jnp.where(lane == 2 * n, sum_one, sums)
        sums = jnp.where(lane == 2 * n + 1, sum_two, sums)
    sums_ref[...] = jnp.broadcast_to(sums, sums_ref.shape)
    high = sums.astype(BF).astype(F32)
    middle = (sums - high).astype(BF).astype(F32)
    low = sums - high - middle
    block = jnp.concatenate([high, middle, low, jnp.zeros((EXTRA - 3, LANES), F32)], axis=0)
    block = jnp.concatenate([block] * (cols // LANES), axis=1).astype(BF)
    for send_ref in send_refs:
        send_ref[tokens:, :] = block


def place_kernel(home_any, mine_ref, *refs):
    got_refs = refs[:3]
    sums_ref, count_ref, update_hbm, pooled_ref, stage_ref, home_ref, sems = refs[3:]
    slots = count_ref.shape[0]
    home_move = pltpu.make_async_copy(home_any, home_ref, sems.at[slots])
    home_move.start()
    tokens = mine_ref.shape[0]
    part = tokens // slots
    width = stage_ref.shape[0] // slots
    head = lax.axis_index("head")
    for n in range(slots):
        for distance, ref in zip(distances(), (mine_ref, *got_refs)):
            start = pl.multiple_of(n * width + (head ^ distance) * part, part)
            stage_ref[pl.ds(start, part), :] = ref[n * part : (n + 1) * part, :].astype(F32)
    home_move.wait()
    moves = []
    for n in range(slots):
        to = pl.ds(pl.multiple_of(home_ref[n] * width, width), width)
        move = pltpu.make_async_copy(
            stage_ref.at[n * width : (n + 1) * width], update_hbm.at[to], sems.at[n]
        )
        move.start()
        moves.append(move)
    sums = sums_ref[0:1, :]
    for ref in got_refs:
        block = ref[tokens:, 0:LANES].astype(F32)
        sums = sums + (block[0:1] + block[1:2] + block[2:3])
    lane = lax.broadcasted_iota(jnp.int32, (1, LANES), 1)
    pooled = jnp.zeros((1, LANES), F32)
    for n in range(slots):
        slot, count = home_ref[n], count_ref[n : n + 1, 0:1]
        pooled = jnp.where(lane == 2 * slot, sums[:, 2 * n : 2 * n + 1] / count, pooled)
        pooled = jnp.where(
            lane == 2 * slot + 1, sums[:, 2 * n + 1 : 2 * n + 2] / (width - count), pooled
        )
    pooled_ref[...] = pooled[:, : pooled_ref.shape[1]]
    for move in moves:
        move.wait()


def call(kernel, out, ins, scratch=(), work=1, **kwargs):
    return pl.pallas_call(
        kernel,
        out_shape=out,
        in_specs=ins,
        scratch_shapes=list(scratch),
        compiler_params=pltpu.CompilerParams(vmem_limit_bytes=LIMIT),
        cost_estimate=pl.CostEstimate(
            flops=int(work * 1e9), bytes_accessed=0, transcendentals=0
        ),
        **kwargs,
    )


def in_hbm(*arrays):
    return [pltpu.with_memory_space_constraint(jnp.asarray(a), pltpu.HBM) for a in arrays]


def partner(value, axis, k):
    count = lax.axis_size(axis)
    return lax.ppermute(value, axis, [(i, i ^ k) for i in range(count)])


def hop(value, even, odd):
    heads, blocks = lax.axis_size("head"), lax.axis_size("blk")
    pairs = []
    for h in range(heads):
        for b in range(blocks):
            pairs.append((h * blocks + b, (h ^ (odd if b % 2 else even)) * blocks + b))
    return lax.ppermute(value, ("head", "blk"), pairs)


def spread_merge(backs, own, pick, slots, bpq):
    cols = backs[0].shape[0] - EXTRA
    width = backs[0].shape[1] // 2
    heads = cols // DH
    parts = jnp.stack(backs).reshape(len(backs), cols + EXTRA, 2, width)
    parts = parts.transpose(0, 2, 1, 3).reshape(2 * len(backs), cols + EXTRA, width)
    order = jnp.argsort(pick, stable=True)
    parts = jnp.take(parts, order, axis=0).reshape(slots, bpq, cols + EXTRA, width)
    stats = parts[:, :, cols : cols + 3 * heads].astype(F32)
    stats = stats.reshape(slots, bpq, 3, heads, width).sum(axis=2)
    stats = jnp.concatenate([stats, own[:, None, cols : cols + heads]], axis=1)
    weight = jnp.exp(stats - jnp.max(stats, axis=1, keepdims=True))
    weight = weight / jnp.sum(weight, axis=1, keepdims=True)
    values = jnp.concatenate([parts[:, :, :cols].astype(F32), own[:, None, :cols]], axis=1)
    values = values.reshape(slots, bpq + 1, heads, DH, width)
    mixed = jnp.sum(values * weight[:, :, :, None, :], axis=1).reshape(slots, cols, width)
    mixed = mixed.transpose(0, 2, 1).astype(BF)
    return [mixed[2 * k : 2 * k + 2].reshape(2 * width, cols) for k in range(slots // 2)]


def body(
    doc_x, doc_seg, doc_query, doc_var, query_len, block_perm, cache_k, cache_v, cache_var,
    w_query, w_key, w_value, w_out, var_bias, norm_gain, readout,
):
    rows, depth = doc_x.shape
    cols = w_query.shape[1]
    blocks = lax.axis_size("blk")
    heads = lax.axis_size("head")
    bpq = blocks // QUERIES
    slots = QUERIES
    width = rows // slots
    chunks = blocks // 2
    order = list(range(chunks))
    cache_rows = cache_k.shape[0]
    seg = doc_seg.reshape(slots, width)
    var = doc_var.reshape(slots, width)
    table = np.concatenate(offset_tables(width), axis=0)
    cache_var = cache_var.reshape(cache_rows // LANES, LANES)
    sds = jax.ShapeDtypeStruct
    i32 = jnp.int32
    chunk_shape = sds((2 * width + EXTRA, cols), BF)
    base_shape = sds((5, slots, width), F32)

    w_first = hop(w_out, 1, 2)

    pick, base, usable, packed, cos, sin, *queries = call(
        functools.partial(query_kernel, bpq, order),
        [
            sds((blocks,), i32), base_shape, sds((8, width), i32),
            sds((2 * cache_rows + EXTRA, cols), BF), sds((rows, LANES), F32),
            sds((rows, LANES), F32),
        ]
        + [chunk_shape] * chunks,
        [HBM] * 11,
        [pltpu.SMEM(ref.shape, i32) for ref in (doc_query, query_len, block_perm)]
        + [pltpu.VMEM(ref.shape, i32) for ref in (seg, var)]
        + [pltpu.VMEM(table.shape, F32), pltpu.VMEM(cache_var.shape, i32)]
        + [pltpu.VMEM(ref.shape, BF) for ref in (cache_v, w_query, doc_x)]
        + [pltpu.VMEM((rows, cols), F32), DMA((11,))],
        out_specs=[SMEM] + [VMEM] * (chunks + 5),
        work=3.5,
        name="query",
    )(
        *in_hbm(
            doc_query, query_len, block_perm, seg, var, table, cache_var, cache_v, cache_k,
            w_query, doc_x,
        )
    )

    asked = [queries[0]] + [partner(queries[k], "blk", 2 * order[k]) for k in range(1, chunks)]
    packed_other = partner(packed, "blk", 1)

    if bpq == 1:
        home = pick
        home_queries = queries
    else:
        home = jnp.arange(slots, dtype=i32)
        every = jnp.stack([q[: 2 * width] for q in queries]).reshape(blocks, width, cols)
        every = jnp.take(every, jnp.argsort(pick, stable=True)[::bpq], axis=0)
        home_queries = [
            every[2 * k : 2 * k + 2].reshape(2 * width, cols) for k in range(slots // 2)
        ]

    own, x_part, count, w_copy = call(
        own_kernel,
        [
            sds((slots, cols + 8, width), F32), sds((rows // heads, depth), BF),
            sds((slots, width), F32), sds(w_out.shape, BF),
        ],
        [ANY] + [VMEM] * (9 + len(home_queries)),
        [
            pltpu.VMEM((rows, cols), F32), pltpu.VMEM((rows, cols), F32),
            pltpu.SMEM(home.shape, i32), DMA,
        ],
        out_specs=[VMEM] * 4,
        work=4.0,
        name="own_documents",
    )(home, var_bias, doc_x, w_key, w_value, var, cos, sin, base, *home_queries, w_first)

    w_second = partner(w_copy, "blk", 1)
    w_third = hop(w_copy, 2, 1)
    parts = []
    for k, query in enumerate(asked):
        after = [parts[-1] if parts else own]
        part = call(
            cache_kernel,
            chunk_shape,
            [VMEM] * 5 + [ANY] * len(after),
            out_specs=VMEM,
            work=1.5,
            name="cache_part",
        )(usable, var_bias, query, packed, packed_other, *after)
        parts.append(part)
    backs = [parts[0]] + [partner(parts[k], "blk", 2 * order[k]) for k in range(1, chunks)]

    def spread(a, b, c):
        return [hop(a, 1, 2), hop(b, 2, 1), partner(c, "head", 3)]

    part_shape = sds((rows // heads // 2, cols), BF)
    halves = []
    if bpq == 1:
        chunk_att = sds((2 * width, cols), BF)
        after, waiting = [parts[-1], w_second, w_third], []
        for group in (range(chunks // 2), range(chunks // 2, chunks)):
            attended = []
            for k in group[:-1]:
                attended.append(
                    call(
                        functools.partial(merge_kernel, k),
                        chunk_att,
                        [VMEM] * 2 + [ANY] * len(after),
                        out_specs=VMEM,
                        work=20 if halves else 0.2,
                        name="merge",
                    )(own, backs[k], *after)
                )
                after = attended[-1:]
            pieces = call(
                functools.partial(last_merge_kernel, group[-1], len(attended)),
                [part_shape] * 4,
                [VMEM] * (2 + len(attended)) + [ANY] * len(after + waiting),
                [pltpu.VMEM(chunk_att.shape, BF)],
                out_specs=[VMEM] * 4,
                work=20 if halves else 0.2,
                name="last_merge",
            )(own, backs[group[-1]], *attended, *after, *waiting)
            halves.append([pieces[0], *spread(*pieces[1:])])
            after, waiting = pieces[:1], halves[-1][1:]
    else:
        attended = spread_merge(backs, own, pick, slots, bpq)
        attended = jnp.concatenate(attended).reshape(slots, width, cols)
        head, part = lax.axis_index("head"), width // heads
        pieces = [
            lax.dynamic_slice_in_dim(attended, (head ^ distance) * part, part, 1)
            for distance in distances()
        ]
        pieces = [piece.reshape(2, *part_shape.shape) for piece in pieces]
        halves = [[piece[i] for piece in pieces] for i in range(2)]
        halves = [[piece, *spread(*others)] for piece, *others in halves]

    gain, read = norm_gain.reshape(1, depth), readout.reshape(1, depth)
    send_shape = sds((rows // heads + EXTRA, cols), BF)
    mine, sums, *sends = call(
        output_kernel,
        [sds((rows // heads, cols), F32), sds((8, LANES), F32)] + [send_shape] * 3,
        [VMEM] * 16,
        [pltpu.VMEM((1, depth), F32)] + [pltpu.VMEM((rows // heads, cols), BF)] * 4,
        out_specs=[VMEM] * 5,
        work=2.0,
        name="output",
    )(
        *halves[0], *halves[1],
        w_out, w_first, w_second, w_third, x_part, count, gain, read,
    )
    update, pooled = call(
        place_kernel,
        [sds((rows, cols), F32), sds((1, 2 * slots), F32)],
        [ANY] + [VMEM] * 6,
        [pltpu.VMEM((rows, cols), F32), pltpu.SMEM(home.shape, i32), DMA((slots + 1,))],
        out_specs=[HBM, VMEM],
        work=1.5,
        name="place",
    )(home, mine, *spread(*sends), sums, count)
    return (update, pooled.reshape(2 * slots))


def solution(mesh):
    return jax.shard_map(
        body,
        mesh=mesh,
        in_specs=(
            P("blk", None), P("blk"), P(), P("blk"), P(), P(), P("blk", "head"),
            P("blk", "head"), P("blk"), P(None, "head"), P(None, "head"), P(None, "head"),
            P("head", None), P(None, "head"), P(), P(),
        ),
        out_specs=(P("blk", "head"), P("blk")),
        check_vma=False,
    )
```

```python
import functools

import jax
import jax.numpy as jnp
import numpy as np
from jax import lax
from jax.experimental import pallas as pl
from jax.experimental.pallas import tpu as pltpu
from jax.sharding import PartitionSpec as P

DH = 64
QUERIES = 8
LANES = 128
EXTRA = 16
NEVER = -1e30
BF = jnp.bfloat16
F32 = jnp.float32
VMEM = pl.BlockSpec(memory_space=pltpu.VMEM)
SMEM = pl.BlockSpec(memory_space=pltpu.SMEM)
HBM = pl.BlockSpec(memory_space=pltpu.HBM)
ANY = pl.BlockSpec(memory_space=pl.ANY)
DMA = pltpu.SemaphoreType.DMA
LIMIT = 32 * 1024 * 1024


def offset_tables(slot_rows):
    half = DH // 2
    freq = (10000.0 ** (-np.arange(half, dtype=np.float64) / half)).astype(np.float32)
    lane_freq = np.tile(freq, LANES // half)
    angles = np.arange(slot_rows, dtype=np.float64)[:, None] * lane_freq[None, :].astype(np.float64)
    sign = np.where(np.arange(LANES) % DH < half, -1.0, 1.0).astype(np.float32)
    rows = np.zeros((8, LANES), np.float32)
    rows[0] = lane_freq
    rows[1] = sign
    return np.cos(angles).astype(np.float32), np.sin(angles).astype(np.float32), rows


def dot(a, b):
    return jnp.dot(a, b, preferred_element_type=F32)


def dot_t(a, b):
    return lax.dot_general(a, b, (((1,), (1,)), ((), ())), preferred_element_type=F32)


def slot_of(p, doc_query, block_perm, slots, bpq):
    blk = lax.axis_index("blk")
    wanted = block_perm[blk ^ p] // bpq
    slot = jnp.int32(0)
    for j in range(slots):
        slot = slot + jnp.where(doc_query[blk * 2 * slots + 2 * j] == wanted, j, 0)
    return slot


def start_tables(doc_query, query_len, seg_ref, rows_ref, base_ref):
    slots, width = seg_ref.shape
    blk = lax.axis_index("blk")
    row = lax.broadcasted_iota(jnp.int32, (slots, width), 0)
    length = jnp.zeros((slots, width), F32)
    for j in range(slots):
        value = query_len[doc_query[blk * 2 * slots + 2 * j]].astype(F32)
        length = jnp.where(row == j, value, length)
    second = (seg_ref[...] & 1).astype(F32)
    count = width - jnp.sum(second, axis=1, keepdims=True)
    count = jnp.broadcast_to(count, (slots, width))
    freq = rows_ref[0:1, :]
    one, two = length * freq, (length - count) * freq
    base_ref[0] = jnp.cos(one)
    base_ref[1] = jnp.sin(one)
    base_ref[2] = jnp.cos(two)
    base_ref[3] = jnp.sin(two)
    base_ref[4] = count


def slot_tables(slot, base_ref, cos_ref, sin_ref, rows_ref):
    shape = cos_ref.shape
    rows = [base_ref[i, pl.ds(slot, 1), :] for i in range(5)]
    token = lax.broadcasted_iota(jnp.int32, shape, 0).astype(F32)
    first = token < rows[4]
    base_cos = jnp.where(first, rows[0], rows[2])
    base_sin = jnp.where(first, rows[1], rows[3])
    off_cos, off_sin = cos_ref[...], sin_ref[...]
    cos = base_cos * off_cos - base_sin * off_sin
    sin = (base_sin * off_cos + base_cos * off_sin) * rows_ref[1:2, :]
    return cos, sin


def turn(value, cos, sin):
    lane = lax.broadcasted_iota(jnp.int32, cos.shape, 1)
    low = lane % DH < DH // 2
    parts = []
    for at in range(0, value.shape[1], LANES):
        part = value[:, at : at + LANES]
        other = jnp.where(
            low, pltpu.roll(part, LANES - DH // 2, 1), pltpu.roll(part, DH // 2, 1)
        )
        parts.append(part * cos + other * sin)
    return jnp.concatenate(parts, axis=1)


def copies(sources, targets, sems):
    moves = [
        pltpu.make_async_copy(source, target, sems.at[i])
        for i, (source, target) in enumerate(zip(sources, targets))
    ]
    for move in moves:
        move.start()
    return moves


def query_kernel(bpq, order, *refs):
    chunks = len(order)
    sources, refs = refs[:11], refs[11:]
    pick_ref, base_ref, usable_ref, packed_ref = refs[:4]
    q_refs, refs = refs[4 : 4 + chunks], refs[4 + chunks :]
    targets, (y_ref, sems) = list(refs[:10]), refs[10:]
    rows, cols = sources[10].shape
    moves = copies(sources, targets + [packed_ref.at[0:rows]], sems)
    doc_query, query_len, block_perm, seg_ref, var_ref, table_ref, key_var_ref = targets[:7]
    x_ref, w_ref, v_ref = targets[7:]
    slots, width = seg_ref.shape
    cos_ref, sin_ref = table_ref.at[0:width], table_ref.at[width : 2 * width]
    rows_ref = table_ref.at[2 * width :]
    for move in moves[:7]:
        move.wait()
    start_tables(doc_query, query_len, seg_ref, rows_ref, base_ref)
    row = lax.broadcasted_iota(jnp.int32, usable_ref.shape, 0)
    usable = jnp.zeros(usable_ref.shape, jnp.int32)
    for j in range(2):
        block = block_perm[lax.axis_index("blk") ^ j]
        here = query_len[block // bpq] - block % bpq * rows
        usable = jnp.where(row == j, here, usable)
    usable_ref[...] = usable
    parts = rows // LANES
    key_var = key_var_ref[...].astype(F32)
    key_var = jnp.concatenate([key_var, jnp.zeros((EXTRA - parts, LANES), F32)], axis=0)
    packed_ref[2 * rows :, :] = jnp.concatenate([key_var, key_var], axis=1).astype(BF)
    for move in moves[7:9]:
        move.wait()
    y_ref[...] = dot(x_ref[...], w_ref[...])
    moves[9].wait()
    for i in range(rows // cols):
        block = v_ref[i * cols : (i + 1) * cols, :].astype(F32)
        packed_ref[rows + i * cols : rows + (i + 1) * cols, :] = block.T.astype(BF)
    for k, q_ref in enumerate(q_refs):
        for j in range(2):
            slot = slot_of(2 * order[k] + j, doc_query, block_perm, slots, bpq)
            pick_ref[2 * k + j] = slot
            cos, sin = slot_tables(slot, base_ref, cos_ref, sin_ref, rows_ref)
            at = pl.ds(pl.multiple_of(slot * width, width), width)
            turned = turn(y_ref[at, :], cos, sin)
            q_ref[j * width : (j + 1) * width, :] = (turned * 0.125).astype(BF)
            var = var_ref[pl.ds(slot, 1), :].astype(F32)
            q_ref[2 * width :, j * width : (j + 1) * width] = jnp.broadcast_to(
                var, (EXTRA, width)
            ).astype(BF)
    moves[10].wait()


def by_head(query):
    lane = lax.broadcasted_iota(jnp.int32, query.shape, 1) // DH
    heads = query.shape[1] // DH
    return jnp.concatenate(
        [jnp.where(lane == h, query, jnp.zeros_like(query)) for h in range(heads)], axis=0
    )


def fold(value, op):
    while value.shape[0] > 8:
        half = value.shape[0] // 2
        value = op(value[:half], value[half:])
    return value


def attend(scores, same, allowed, bias_ref, values, out_ref, at):
    width = same.shape[1]
    stats = []
    for h in range(scores.shape[1] // width):
        part = scores[:, h * width : (h + 1) * width]
        part = part + jnp.where(same, bias_ref[0:1, h : h + 1], bias_ref[1:2, h : h + 1])
        part = jnp.where(allowed, part, NEVER)
        peak = jnp.max(fold(part, jnp.maximum), axis=0, keepdims=True)
        weight = jnp.exp(part - peak)
        total = jnp.sum(fold(weight, jnp.add), axis=0, keepdims=True)
        weight = weight.astype(BF)
        mixed = None
        key = 0
        for value in values:
            keys = value.shape[1]
            term = dot(value[h * DH : (h + 1) * DH, :], weight[key : key + keys, :])
            mixed = term if mixed is None else mixed + term
            key += keys
        mixed = mixed * (1.0 / total)
        out_ref[h * DH : (h + 1) * DH, at] = mixed.astype(out_ref.dtype)
        stats.append(peak + jnp.log(total))
    return stats


def cache_kernel(usable_ref, bias_ref, q_ref, own_ref, other_ref, *refs):
    out_ref = refs[-1]
    width = q_ref.shape[0] // 2 - EXTRA // 2
    cols = q_ref.shape[1]
    rows = (own_ref.shape[0] - EXTRA) // 2
    for j, ref in enumerate((own_ref, other_ref)):
        var = ref[2 * rows :, 0:LANES].astype(F32)
        var = jnp.concatenate([var, jnp.zeros((LANES - EXTRA, LANES), F32)], axis=0).T
        key_var = jnp.concatenate(
            [jnp.broadcast_to(var[:, i : i + 1], (LANES, width)) for i in range(rows // LANES)],
            axis=0,
        )
        tok_var = q_ref[2 * width :, j * width : (j + 1) * width].astype(F32)[0:1, :]
        same = key_var == tok_var
        allowed = lax.broadcasted_iota(jnp.int32, (rows, width), 0) < usable_ref[j : j + 1, :]
        scores = dot_t(ref[0:rows, :], by_head(q_ref[j * width : (j + 1) * width, :]))
        values = [ref[rows + i * cols : rows + (i + 1) * cols, :] for i in range(rows // cols)]
        at = slice(j * width, (j + 1) * width)
        stats = attend(scores, same, allowed, bias_ref, values, out_ref, at)
        full = jnp.concatenate(stats, axis=0)
        high = full.astype(BF).astype(F32)
        middle = (full - high).astype(BF).astype(F32)
        low = full - high - middle
        pad = jnp.zeros((EXTRA - 3 * len(stats), width), F32)
        out_ref[cols:, at] = jnp.concatenate([high, middle, low, pad], axis=0).astype(BF)


def own_kernel(
    home_any, bias_ref, x_ref, wk_ref, wv_ref, var_ref, table_ref, base_ref,
    *refs
):
    w_ref, out_ref, x_part_ref, count_ref, w_copy_ref, k_ref, v_ref, home_ref, sem = refs[-9:]
    q_refs = refs[:-9]
    part = x_part_ref.shape[0] // var_ref.shape[0]
    part_start = lax.axis_index("head") * part
    w_copy_ref[...] = w_ref[...]
    slots, width = var_ref.shape
    cols = wk_ref.shape[1]
    home_move = pltpu.make_async_copy(home_any, home_ref, sem)
    home_move.start()
    cos_ref, sin_ref = table_ref.at[0:width], table_ref.at[width : 2 * width]
    rows_ref = table_ref.at[2 * width :]
    k_ref[...] = dot(x_ref[...], wk_ref[...])
    v_ref[...] = dot(x_ref[...], wv_ref[...])
    home_move.wait()
    for n in range(slots):
        slot = home_ref[n]
        cos, sin = slot_tables(slot, base_ref, cos_ref, sin_ref, rows_ref)
        at = pl.ds(pl.multiple_of(slot * width, width), width)
        part_at = pl.ds(pl.multiple_of(slot * width + part_start, part), part)
        x_part_ref[n * part : (n + 1) * part, :] = x_ref[part_at, :]
        key = turn(k_ref[at, :], cos, sin).astype(BF)
        value = v_ref[at, :].T.astype(BF)
        query = q_refs[n // 2][n % 2 * width : (n % 2 + 1) * width, :]
        scores = dot_t(key, by_head(query))
        var = jnp.broadcast_to(var_ref[pl.ds(slot, 1), :].astype(F32), (width, width))
        same = var.T == var
        count = base_ref[4, pl.ds(slot, 1), :]
        count_ref[n : n + 1, :] = count
        key_second = lax.broadcasted_iota(jnp.int32, (width, width), 0).astype(F32) >= count
        tok_second = lax.broadcasted_iota(jnp.int32, (width, width), 1).astype(F32) >= count
        allowed = jnp.logical_not(jnp.logical_xor(key_second, tok_second))
        part_ref = out_ref.at[n]
        stats = attend(scores, same, allowed, bias_ref, [value], part_ref, slice(None))
        stats = jnp.concatenate(stats + [jnp.zeros((8 - len(stats), width), F32)], axis=0)
        part_ref[cols:, :] = stats


def distances():
    core = lax.axis_index("blk") % 2
    return [0, 1 + core, 2 - core, 3]


def merge(first, got_ref, own_ref, out_ref, start):
    cols = got_ref.shape[0] - EXTRA
    heads = cols // DH
    width = got_ref.shape[1] // 2
    for j in range(2):
        at = slice(j * width, (j + 1) * width)
        stats = got_ref[cols:, at].astype(F32)
        there = stats[0:heads] + stats[heads : 2 * heads] + stats[2 * heads : 3 * heads]
        here = own_ref[first + j, cols : cols + heads, :]
        peak = jnp.maximum(there, here)
        there, here = jnp.exp(there - peak), jnp.exp(here - peak)
        inverse = 1.0 / (there + here)
        there, here = there * inverse, here * inverse
        parts = []
        for h in range(heads):
            row = slice(h * DH, (h + 1) * DH)
            parts.append(
                got_ref[row, at].astype(F32) * there[h : h + 1]
                + own_ref[first + j, row, :] * here[h : h + 1]
            )
        to = slice(start + j * width, start + (j + 1) * width)
        out_ref[to, :] = jnp.concatenate(parts, axis=0).T.astype(BF)


def merge_kernel(chunk, own_ref, got_ref, *refs):
    out_ref = refs[-1]
    merge(2 * chunk, got_ref, own_ref, out_ref, 0)


def last_merge_kernel(chunk, earlier, own_ref, got_ref, *refs):
    att_refs = [*refs[:earlier], refs[-1]]
    out_refs = refs[-5:-1]
    merge(2 * chunk, got_ref, own_ref, refs[-1], 0)
    slots = 2 * len(att_refs)
    width = refs[-1].shape[0] // 2
    part = out_refs[0].shape[0] // slots
    head = lax.axis_index("head")
    for distance, out_ref in zip(distances(), out_refs):
        for n in range(slots):
            start = pl.multiple_of(n % 2 * width + (head ^ distance) * part, part)
            out_ref[n * part : (n + 1) * part, :] = att_refs[n // 2][pl.ds(start, part), :]


def output_kernel(*refs):
    att_halves, refs = (refs[0:4], refs[4:8]), refs[8:]
    w_refs = refs[:4]
    x_ref, count_ref, gain_ref, read_ref = refs[4:8]
    mine_ref, sums_ref = refs[8:10]
    send_refs, gr_ref, att_refs = refs[10:13], refs[13], refs[14:]
    for first_ref, second_ref, att_ref in zip(*att_halves, att_refs):
        att_ref[0 : first_ref.shape[0], :] = first_ref[...]
        att_ref[first_ref.shape[0] :, :] = second_ref[...]
    tokens, cols = att_refs[0].shape
    depth = w_refs[0].shape[1]
    slots = count_ref.shape[0]
    part = tokens // slots
    gr_ref[...] = gain_ref[...] * read_ref[...]
    head = lax.axis_index("head")
    square = jnp.zeros((tokens, LANES), F32)
    weighted = jnp.zeros((tokens, LANES), F32)
    for c, distance in enumerate(distances()):
        at = pl.ds(pl.multiple_of((head ^ distance) * cols, cols), cols)
        total = dot(att_refs[0][...], w_refs[0][:, at])
        for att_ref, w_ref in zip(att_refs[1:], w_refs[1:]):
            total = total + dot(att_ref[...], w_ref[:, at])
        if c == 0:
            mine_ref[...] = total
        else:
            send_refs[c - 1][0:tokens, :] = total.astype(BF)
        hidden = x_ref[:, at].astype(F32) + total
        scaled = hidden * gr_ref[:, at]
        hidden = hidden * hidden
        for lane in range(0, cols, LANES):
            square = square + hidden[:, lane : lane + LANES]
            weighted = weighted + scaled[:, lane : lane + LANES]
    square = jnp.sum(square, axis=1, keepdims=True)
    weighted = jnp.sum(weighted, axis=1, keepdims=True)
    score = weighted * lax.rsqrt(square / depth + 1e-06)
    token = lax.broadcasted_iota(jnp.int32, (part, 1), 0) + head * part
    lane = lax.broadcasted_iota(jnp.int32, (1, LANES), 1)
    sums = jnp.zeros((1, LANES), F32)
    for n in range(slots):
        is_first = token.astype(F32) < count_ref[n : n + 1, 0:1]
        piece = score[n * part : (n + 1) * part, :]
        sum_one = jnp.sum(jnp.where(is_first, piece, 0.0), axis=0, keepdims=True)
        sum_two = jnp.sum(jnp.where(is_first, 0.0, piece), axis=0, keepdims=True)
        sums = jnp.where(lane == 2 * n, sum_one, sums)
        sums = jnp.where(lane == 2 * n + 1, sum_two, sums)
    sums_ref[...] = jnp.broadcast_to(sums, sums_ref.shape)
    high = sums.astype(BF).astype(F32)
    middle = (sums - high).astype(BF).astype(F32)
    low = sums - high - middle
    block = jnp.concatenate([high, middle, low, jnp.zeros((EXTRA - 3, LANES), F32)], axis=0)
    block = jnp.concatenate([block] * (cols // LANES), axis=1).astype(BF)
    for send_ref in send_refs:
        send_ref[tokens:, :] = block


def place_kernel(home_any, mine_ref, *refs):
    got_refs = refs[:3]
    sums_ref, count_ref, update_hbm, pooled_ref, stage_ref, home_ref, sems = refs[3:]
    slots = count_ref.shape[0]
    home_move = pltpu.make_async_copy(home_any, home_ref, sems.at[slots])
    home_move.start()
    tokens = mine_ref.shape[0]
    part = tokens // slots
    width = stage_ref.shape[0] // slots
    head = lax.axis_index("head")
    sums = sums_ref[0:1, :]
    for ref in got_refs:
        block = ref[tokens:, 0:LANES].astype(F32)
        sums = sums + (block[0:1] + block[1:2] + block[2:3])
    moves = []
    for n in range(slots):
        for distance, ref in zip(distances(), (mine_ref, *got_refs)):
            start = pl.multiple_of(n * width + (head ^ distance) * part, part)
            stage_ref[pl.ds(start, part), :] = ref[n * part : (n + 1) * part, :].astype(F32)
        if n == 0:
            home_move.wait()
        to = pl.ds(pl.multiple_of(home_ref[n] * width, width), width)
        move = pltpu.make_async_copy(
            stage_ref.at[n * width : (n + 1) * width], update_hbm.at[to], sems.at[n]
        )
        move.start()
        moves.append(move)
    lane = lax.broadcasted_iota(jnp.int32, (1, LANES), 1)
    pooled = jnp.zeros((1, LANES), F32)
    for n in range(slots):
        slot, count = home_ref[n], count_ref[n : n + 1, 0:1]
        pooled = jnp.where(lane == 2 * slot, sums[:, 2 * n : 2 * n + 1] / count, pooled)
        pooled = jnp.where(
            lane == 2 * slot + 1, sums[:, 2 * n + 1 : 2 * n + 2] / (width - count), pooled
        )
    pooled_ref[...] = pooled[:, : pooled_ref.shape[1]]
    for move in moves:
        move.wait()


def call(kernel, out, ins, scratch=(), work=1, **kwargs):
    return pl.pallas_call(
        kernel,
        out_shape=out,
        in_specs=ins,
        scratch_shapes=list(scratch),
        compiler_params=pltpu.CompilerParams(vmem_limit_bytes=LIMIT),
        cost_estimate=pl.CostEstimate(
            flops=int(work * 1e9), bytes_accessed=0, transcendentals=0
        ),
        **kwargs,
    )


def in_hbm(*arrays):
    return [pltpu.with_memory_space_constraint(jnp.asarray(a), pltpu.HBM) for a in arrays]


def partner(value, axis, k):
    count = lax.axis_size(axis)
    return lax.ppermute(value, axis, [(i, i ^ k) for i in range(count)])


def hop(value, even, odd):
    heads, blocks = lax.axis_size("head"), lax.axis_size("blk")
    pairs = []
    for h in range(heads):
        for b in range(blocks):
            pairs.append((h * blocks + b, (h ^ (odd if b % 2 else even)) * blocks + b))
    return lax.ppermute(value, ("head", "blk"), pairs)


def spread_merge(backs, own, pick, slots, bpq):
    cols = backs[0].shape[0] - EXTRA
    width = backs[0].shape[1] // 2
    heads = cols // DH
    parts = jnp.stack(backs).reshape(len(backs), cols + EXTRA, 2, width)
    parts = parts.transpose(0, 2, 1, 3).reshape(2 * len(backs), cols + EXTRA, width)
    order = jnp.argsort(pick, stable=True)
    parts = jnp.take(parts, order, axis=0).reshape(slots, bpq, cols + EXTRA, width)
    stats = parts[:, :, cols : cols + 3 * heads].astype(F32)
    stats = stats.reshape(slots, bpq, 3, heads, width).sum(axis=2)
    stats = jnp.concatenate([stats, own[:, None, cols : cols + heads]], axis=1)
    weight = jnp.exp(stats - jnp.max(stats, axis=1, keepdims=True))
    weight = weight / jnp.sum(weight, axis=1, keepdims=True)
    values = jnp.concatenate([parts[:, :, :cols].astype(F32), own[:, None, :cols]], axis=1)
    values = values.reshape(slots, bpq + 1, heads, DH, width)
    mixed = jnp.sum(values * weight[:, :, :, None, :], axis=1).reshape(slots, cols, width)
    mixed = mixed.transpose(0, 2, 1).astype(BF)
    return [mixed[2 * k : 2 * k + 2].reshape(2 * width, cols) for k in range(slots // 2)]


def body(
    doc_x, doc_seg, doc_query, doc_var, query_len, block_perm, cache_k, cache_v, cache_var,
    w_query, w_key, w_value, w_out, var_bias, norm_gain, readout,
):
    rows, depth = doc_x.shape
    cols = w_query.shape[1]
    blocks = lax.axis_size("blk")
    heads = lax.axis_size("head")
    bpq = blocks // QUERIES
    slots = QUERIES
    width = rows // slots
    chunks = blocks // 2
    order = list(range(chunks))
    cache_rows = cache_k.shape[0]
    seg = doc_seg.reshape(slots, width)
    var = doc_var.reshape(slots, width)
    table = np.concatenate(offset_tables(width), axis=0)
    cache_var = cache_var.reshape(cache_rows // LANES, LANES)
    sds = jax.ShapeDtypeStruct
    i32 = jnp.int32
    chunk_shape = sds((2 * width + EXTRA, cols), BF)
    base_shape = sds((5, slots, width), F32)

    w_first = hop(w_out, 1, 2)

    pick, base, usable, packed, *queries = call(
        functools.partial(query_kernel, bpq, order),
        [
            sds((blocks,), i32), base_shape, sds((8, width), i32),
            sds((2 * cache_rows + EXTRA, cols), BF),
        ]
        + [chunk_shape] * chunks,
        [HBM] * 11,
        [pltpu.SMEM(ref.shape, i32) for ref in (doc_query, query_len, block_perm)]
        + [pltpu.VMEM(ref.shape, i32) for ref in (seg, var)]
        + [pltpu.VMEM(table.shape, F32), pltpu.VMEM(cache_var.shape, i32)]
        + [pltpu.VMEM(ref.shape, BF) for ref in (doc_x, w_query, cache_v)]
        + [pltpu.VMEM((rows, cols), F32), DMA((11,))],
        out_specs=[SMEM] + [VMEM] * (chunks + 3),
        work=3.5,
        name="query",
    )(
        *in_hbm(
            doc_query, query_len, block_perm, seg, var, table, cache_var, doc_x, w_query,
            cache_v, cache_k,
        )
    )

    asked = [queries[0]] + [partner(queries[k], "blk", 2 * order[k]) for k in range(1, chunks)]
    packed_other = partner(packed, "blk", 1)

    if bpq == 1:
        home = pick
        home_queries = queries
    else:
        home = jnp.arange(slots, dtype=i32)
        every = jnp.stack([q[: 2 * width] for q in queries]).reshape(blocks, width, cols)
        every = jnp.take(every, jnp.argsort(pick, stable=True)[::bpq], axis=0)
        home_queries = [
            every[2 * k : 2 * k + 2].reshape(2 * width, cols) for k in range(slots // 2)
        ]

    own, x_part, count, w_copy = call(
        own_kernel,
        [
            sds((slots, cols + 8, width), F32), sds((rows // heads, depth), BF),
            sds((slots, width), F32), sds(w_out.shape, BF),
        ],
        [ANY] + [VMEM] * (8 + len(home_queries)),
        [
            pltpu.VMEM((rows, cols), F32), pltpu.VMEM((rows, cols), F32),
            pltpu.SMEM(home.shape, i32), DMA,
        ],
        out_specs=[VMEM] * 4,
        work=4.0,
        name="own_documents",
    )(home, var_bias, doc_x, w_key, w_value, var, table, base, *home_queries, w_first)

    w_second = partner(w_copy, "blk", 1)
    w_third = hop(w_copy, 2, 1)
    parts = []
    for k, query in enumerate(asked):
        after = [parts[-1] if parts else own]
        part = call(
            cache_kernel,
            chunk_shape,
            [VMEM] * 5 + [ANY] * len(after),
            out_specs=VMEM,
            work=1.5,
            name="cache_part",
        )(usable, var_bias, query, packed, packed_other, *after)
        parts.append(part)
    backs = [parts[0]] + [partner(parts[k], "blk", 2 * order[k]) for k in range(1, chunks)]

    def spread(a, b, c):
        return [hop(a, 1, 2), hop(b, 2, 1), partner(c, "head", 3)]

    part_shape = sds((rows // heads // 2, cols), BF)
    halves = []
    if bpq == 1:
        chunk_att = sds((2 * width, cols), BF)
        after, waiting = [parts[-1], w_second, w_third], []
        for group in (range(chunks // 2), range(chunks // 2, chunks)):
            attended = []
            for k in group[:-1]:
                attended.append(
                    call(
                        functools.partial(merge_kernel, k),
                        chunk_att,
                        [VMEM] * 2 + [ANY] * len(after),
                        out_specs=VMEM,
                        work=20 if halves else 0.2,
                        name="merge",
                    )(own, backs[k], *after)
                )
                after = attended[-1:]
            pieces = call(
                functools.partial(last_merge_kernel, group[-1], len(attended)),
                [part_shape] * 4,
                [VMEM] * (2 + len(attended)) + [ANY] * len(after + waiting),
                [pltpu.VMEM(chunk_att.shape, BF)],
                out_specs=[VMEM] * 4,
                work=20 if halves else 0.2,
                name="last_merge",
            )(own, backs[group[-1]], *attended, *after, *waiting)
            halves.append([pieces[0], *spread(*pieces[1:])])
            after, waiting = pieces[:1], halves[-1][1:]
    else:
        attended = spread_merge(backs, own, pick, slots, bpq)
        attended = jnp.concatenate(attended).reshape(slots, width, cols)
        head, part = lax.axis_index("head"), width // heads
        pieces = [
            lax.dynamic_slice_in_dim(attended, (head ^ distance) * part, part, 1)
            for distance in distances()
        ]
        pieces = [piece.reshape(2, *part_shape.shape) for piece in pieces]
        halves = [[piece[i] for piece in pieces] for i in range(2)]
        halves = [[piece, *spread(*others)] for piece, *others in halves]

    gain, read = norm_gain.reshape(1, depth), readout.reshape(1, depth)
    send_shape = sds((rows // heads + EXTRA, cols), BF)
    mine, sums, *sends = call(
        output_kernel,
        [sds((rows // heads, cols), F32), sds((8, LANES), F32)] + [send_shape] * 3,
        [VMEM] * 16,
        [pltpu.VMEM((1, depth), F32)] + [pltpu.VMEM((rows // heads, cols), BF)] * 4,
        out_specs=[VMEM] * 5,
        work=2.0,
        name="output",
    )(
        *halves[0], *halves[1],
        w_out, w_first, w_second, w_third, x_part, count, gain, read,
    )
    update, pooled = call(
        place_kernel,
        [sds((rows, cols), F32), sds((1, 2 * slots), F32)],
        [ANY] + [VMEM] * 6,
        [pltpu.VMEM((rows, cols), F32), pltpu.SMEM(home.shape, i32), DMA((slots + 1,))],
        out_specs=[HBM, VMEM],
        work=1.5,
        name="place",
    )(home, mine, *spread(*sends), sums, count)
    return (update, pooled.reshape(2 * slots))


def solution(mesh):
    return jax.shard_map(
        body,
        mesh=mesh,
        in_specs=(
            P("blk", None), P("blk"), P(), P("blk"), P(), P(), P("blk", "head"),
            P("blk", "head"), P("blk"), P(None, "head"), P(None, "head"), P(None, "head"),
            P("head", None), P(None, "head"), P(), P(),
        ),
        out_specs=(P("blk", "head"), P("blk")),
        check_vma=False,
    )
```
